512 devices in a mesh: gx: 8 (over y, core), yz: 64 (over x, z).
Axes of the slice: x: 4, y: 4, z: 16, core: 2. Of those that a mesh axis runs over, the one named last changes fastest.
Arguments:
- right_side: float32 [128, 2048, 128], P('gx', 'yz'), may hold values from -6 to 6
- coefficient: float32 [128, 2048, 128], P('gx', 'yz'), may hold values from 0.5 to 8
Outputs:
- solution: float32 [128, 2048, 128], P('gx', 'yz')
The draws below stay inside these ranges and needn't reach their ends.
All inputs are finite; a program needn't handle non-finite values.
Results may differ from the reference program's by a relative error of at most 0.0001.
Values sent between devices are 32-bit elements; how exact they have to be, the bound alone decides.
A program may use at most 64 MiB of HBM per device.

```python
import math
import jax
import jax.numpy as jnp

CZ = 128
LEVELS = 4
BITERS = 4
NX = 128
NY = 2048


def level_of(stream_key, extent, cuts, smallest, largest):
    def one(dim, shards_of):
        draws = jax.random.uniform(jax.random.fold_in(jax.random.fold_in(stream_key, 6), dim), (shards_of,), jnp.float32, smallest / len(cuts), largest / len(cuts))
        return jnp.repeat(jnp.exp(draws), extent[dim] // shards_of).reshape((-1,) + (1,) * (len(extent) - dim - 1))

    gain = one(*cuts[0])
    for cut in cuts[1:]:
        gain = gain * one(*cut)
    return gain


def gaussian(stream_key, dims, width, limit, shards=(), kind=jnp.bfloat16):
    values = jax.random.normal(stream_key, dims, jnp.float32) * width
    if len(shards) > 0:
        values = level_of(stream_key, dims, shards, -0.22, 0.18) * values
    return jnp.clip(values, min=-limit, max=limit).astype(kind)


def setup_inputs(seed: int = 0) -> dict:
    key_of = jax.random.split(jax.random.key(seed), 3)
    return {
        "right_side": gaussian(key_of[0], (NX, NY, CZ), 1.0, 6.0, ((0, 8), (1, 64)), jnp.float32),
        "coefficient": jnp.clip(jnp.exp(math.log(8.0) - 2.7725887 * jax.random.uniform(key_of[1], (NX, NY, CZ), jnp.float32) ** level_of(key_of[1], (NX, NY, CZ), ((0, 8), (1, 64)), -0.2, 0.2)), 0.5, 8.0),
    }


RELAXATION = 0.8


def neighbours(padded):
    return [padded[2:, 1:-1, 1:-1], padded[:-2, 1:-1, 1:-1],
            padded[1:-1, 2:, 1:-1], padded[1:-1, :-2, 1:-1],
            padded[1:-1, 1:-1, 2:], padded[1:-1, 1:-1, :-2]]


def face_weights(padded):
    centre = padded[1:-1, 1:-1, 1:-1]
    return [0.5 * (centre + other) for other in neighbours(padded)]


def diagonal_of(face_list, level_scale):
    summed = face_list[0]
    for weight in face_list[1:]:
        summed = summed + weight
    return level_scale * summed


def operate(padded, face_list, level_scale):
    centre = padded[1:-1, 1:-1, 1:-1]
    others = neighbours(padded)
    summed = face_list[0] * (centre - others[0])
    for position in range(1, 6):
        summed = summed + face_list[position] * (centre - others[position])
    return level_scale * summed


def restrict(values):
    return values.reshape(values.shape[0] // 2, 2, values.shape[1] // 2, 2, values.shape[2] // 2, 2).mean(axis=(1, 3, 5))


def prolong(values):
    return jnp.repeat(jnp.repeat(jnp.repeat(values, 2, 0), 2, 1), 2, 2)


def stabilized_solve(source, weight):
    level_scale = 0.25 ** LEVELS
    face_list = face_weights(jnp.pad(weight, 1))

    def apply_op(values):
        return operate(jnp.pad(values, 1), face_list, level_scale)

    answer = jnp.zeros_like(source)
    residual = source
    shadow = source
    rho_now = jnp.sum(shadow * residual)
    rho_prev = rho_now
    direction = residual
    applied = jnp.zeros_like(source)
    step_alpha = jnp.float32(1.0)
    step_omega = jnp.float32(1.0)
    for turn_index in range(BITERS):
        if turn_index > 0:
            beta_factor = (rho_now / rho_prev) * (step_alpha / step_omega)
            direction = residual + beta_factor * (direction - step_omega * applied)
        applied = apply_op(direction)
        step_alpha = rho_now / jnp.sum(shadow * applied)
        middle = residual - step_alpha * applied
        bent_image = apply_op(middle)
        step_omega = jnp.sum(bent_image * middle) / jnp.sum(bent_image * bent_image)
        answer = answer + step_alpha * direction + step_omega * middle
        residual = middle - step_omega * bent_image
        if turn_index + 1 < BITERS:
            rho_prev = rho_now
            rho_now = jnp.sum(shadow * residual)
    return answer


def reference(right_side, coefficient):
    source = right_side
    weight = coefficient
    stored = []
    for level_index in range(LEVELS):
        level_scale = 0.25 ** level_index
        face_list = face_weights(jnp.pad(weight, 1))
        diagonal = diagonal_of(face_list, level_scale)
        iterate = RELAXATION * source / diagonal
        iterate = iterate + RELAXATION * (source - operate(jnp.pad(iterate, 1), face_list, level_scale)) / diagonal
        residual = source - operate(jnp.pad(iterate, 1), face_list, level_scale)
        stored.append((source, iterate, weight))
        source = restrict(residual)
        weight = restrict(weight)
    correction = stabilized_solve(source, weight)
    for level_index in reversed(range(LEVELS)):
        source, iterate, weight = stored[level_index]
        level_scale = 0.25 ** level_index
        face_list = face_weights(jnp.pad(weight, 1))
        diagonal = diagonal_of(face_list, level_scale)
        iterate = iterate + prolong(correction)
        iterate = iterate + RELAXATION * (source - operate(jnp.pad(iterate, 1), face_list, level_scale)) / diagonal
        correction = iterate
    return correction
```

```python
import jax
import jax.numpy as jnp
from jax import lax
from jax.experimental import pallas as pl
from jax.experimental.pallas import tpu as pltpu
from jax.sharding import PartitionSpec as P

MESH = pl.DeviceIdType.MESH
BITERS = 4
OMEGA = 0.8
NG = 8
NQ = 64
F32 = jnp.float32


def roll(v, by):
    return pltpu.roll(v, by % 128, 1)


def lanes_of(rows):
    return lax.broadcasted_iota(jnp.int32, (rows, 128), 1)


def swap(v, bit):
    lane = lanes_of(v.shape[0])
    return jnp.where((lane & bit) == 0, roll(v, -bit), roll(v, bit))


class Level:
    def __init__(self, scale, rows, start, count, unit, planes, depth, pieces):
        self.half = 0.5 * scale
        self.rows = rows
        self.start = start
        self.unit = unit
        self.planes = planes
        self.depth = depth

    def load(self, ref, i, shift=0):
        return ref[i, pl.ds(self.start + shift, self.rows), :]

    def store(self, ref, i, v):
        ref[i, pl.ds(self.start, self.rows), :] = v

    def shifted(self, ref, i):
        c = self.load(ref, i)
        if self.planes == 1:
            xp, xm = self.load(ref, i + 1), self.load(ref, i - 1)
        else:
            n, s = self.planes, self.unit
            field = (lanes_of(self.rows) // s) & (n - 1)
            xp = jnp.where(field < n - 1, roll(c, -s), roll(self.load(ref, i + 1), (n - 1) * s))
            xm = jnp.where(field > 0, roll(c, s), roll(self.load(ref, i - 1), -(n - 1) * s))
        yp, ym = self.load(ref, i, 1), self.load(ref, i, -1)
        zp, zm = roll(c, -self.depth), roll(c, self.depth)
        return c, (xp, xm, yp, ym, zp, zm)

    def weigh(self, i):
        lane = lanes_of(self.rows)
        first, last = lane < self.depth, lane >= 128 - self.depth
        c, others = self.shifted(self.b, i)
        total = None
        for k, other in enumerate(others):
            edge = {4: last, 5: first}.get(k)
            if edge is not None:
                other = jnp.where(edge, 0.0, other)
            w = self.half * (c + other)
            total = w if total is None else total + w
            if edge is not None:
                w = jnp.where(edge, 0.0, w)
            self.w[k, i, pl.ds(self.start, self.rows), :] = w
        self.store(self.d, i, total)
        inside = c > 0.0
        self.store(self.inv, i, jnp.where(inside, OMEGA / jnp.where(inside, total, 1.0), 0.0))

    def first(self, i):
        self.store(self.v, i, self.load(self.inv, i) * self.load(self.f, i))

    def around(self, ref, i):
        c, others = self.shifted(ref, i)
        total = None
        for k, other in enumerate(others):
            term = self.w[k, i, pl.ds(self.start, self.rows), :] * other
            total = term if total is None else total + term
        return c, total

    def smooth(self, src, i):
        c, s = self.around(src, i)
        return (1.0 - OMEGA) * c + self.load(self.inv, i) * (self.load(self.f, i) + s)

    def residual(self, i):
        c, s = self.around(self.u, i)
        return self.load(self.f, i) + s - self.load(self.d, i) * c


def each(lo, hi, body, group=None):
    if group is None:
        for i in range(lo, hi):
            body(i)
    else:
        assert (hi - lo) % group == 0

        def step(t, carry):
            for k in range(group):
                body(lo + t * group + k)
            return carry

        lax.fori_loop(0, (hi - lo) // group, step, 0)


R0, O0 = 56, 12
R1, O1 = 40, 12
R2, O2 = 40, 16
R3, O3 = 32, 16

LEVEL_SHAPES = ((22, R0), (10, R1), (10, R2), (10, R3))


def kernel(f_hbm, b_hbm, out, *refs):
    refs = list(refs)

    def take(n):
        got = refs[:n]
        del refs[:n]
        return got

    lv = [
        Level(1.0, 40, 8, 16, 1, 1, 1, 1),
        Level(0.25, 24, 8, 4, 1, 2, 2, 1),
        Level(0.0625, 24, 8, 8, 1, 4, 4, 1),
        Level(0.015625, 16, 8, 8, 2, 2, 8, 1),
    ]
    for one in lv:
        one.b, one.f, one.v, one.u, one.d, one.inv, one.w = take(7)
    pair, b2_own, f2_own, gathered, e_pad = take(5)
    load_sem, send_sem, near_recv, wide_recv, far_recv = take(5)
    l0, l1, l2, l3 = lv

    g, q = lax.axis_index("gx"), lax.axis_index("yz")

    load_b = pltpu.make_async_copy(b_hbm, l0.b.at[pl.ds(3, 16), pl.ds(O0, 32)], load_sem.at[0])
    load_f = pltpu.make_async_copy(f_hbm, l0.f.at[pl.ds(3, 16), pl.ds(O0, 32)], load_sem.at[1])
    load_b.start()
    load_f.start()

    def device(dg, dq):
        return {"gx": lax.rem(g + dg + NG, NG), "yz": lax.rem(q + dq + NQ, NQ)}

    near = [(dg, dq) for dg in (-1, 0, 1) for dq in (-1, 0, 1) if dg or dq]
    wide = [(dg, dq) for dg in (4, 3, 5, 2, 6, 1, 7, 0) for dq in (-1, 1, 0) if dg or dq]

    def yz_order():
        order = []
        for d in range(1, NQ):
            z, x = d % 16, d // 16
            order.append((-(min(z, 16 - z) + min(x, 4 - x)), d))
        return [d for _, d in sorted(order)]

    far = yz_order()

    barrier = pltpu.get_barrier_semaphore()

    def greet(target):
        pl.semaphore_signal(barrier, inc=1, device_id=target, device_id_type=MESH)

    for d in far:
        if d not in (1, NQ - 1):
            greet(device(0, d))
    for dg, dq in wide:
        greet(device(dg, dq))

    for one, (blocks, rows) in ((l1, LEVEL_SHAPES[1]), (l2, LEVEL_SHAPES[2]), (l3, LEVEL_SHAPES[3])):
        for ref in (one.b, one.v, one.u):
            for i in (0, blocks - 1):
                ref[i] = jnp.zeros((rows, 128), F32)
    for ref in (l3.b, l3.f):
        for i in range(1, 9):
            ref[i] = jnp.zeros((R3, 128), F32)
    e_pad[pl.ds(0, 8), :] = jnp.zeros((8, 128), F32)
    e_pad[pl.ds(72, 8), :] = jnp.zeros((8, 128), F32)

    even = (lanes_of(16) & 1) == 0

    def restrict_0(make, store):
        def body(i):
            halves = []
            for half in range(2):
                slot = 2 * i + half
                pair[slot, pl.ds(0, 32), :] = make(2 * slot) + make(2 * slot + 1)
                t = pair[slot, pl.ds(0, 16, stride=2), :] + pair[slot, pl.ds(1, 16, stride=2), :]
                halves.append(t + swap(t, 1))
            store(i, 0.125 * jnp.where(even, halves[0], halves[1]))

        return body

    def restrict_1(make, rows):
        lane = lanes_of(rows)
        packed = None
        for i in range(4):
            pair[i, pl.ds(0, 2 * rows), :] = make(i)
            t = pair[i, pl.ds(0, rows, stride=2), :] + pair[i, pl.ds(1, rows, stride=2), :]
            t = t + swap(t, 1)
            t = t + swap(t, 2)
            packed = t if packed is None else jnp.where((lane & 3) == i, t, packed)
        return 0.125 * packed

    def restrict_2(make):
        def one(i):
            pair[i, pl.ds(0, 24), :] = make(i)
            t = pair[i, pl.ds(0, 12, stride=2), :] + pair[i, pl.ds(1, 12, stride=2), :]
            t = t + swap(t, 1)
            return 0.125 * (t + swap(t, 4))

        return one

    def restrict_3(make):
        k = lanes_of(1) & 15
        row = None
        for i in range(8):
            pair[i, pl.ds(0, 4), :] = make(i)
            t = pair[i, pl.ds(0, 2, stride=2), :] + pair[i, pl.ds(1, 2, stride=2), :]
            t = t + swap(t, 2)
            t = 0.125 * (t + swap(t, 8))
            for j in range(2):
                row = t[j : j + 1] if row is None else jnp.where(k == 2 * i + j, t[j : j + 1], row)
        return row

    load_b.wait()

    def store_b1(i, v):
        l1.b[3 + i, pl.ds(O1, 16), :] = v

    each(0, 4, restrict_0(lambda p: l0.b[3 + p, pl.ds(O0, 32), :], store_b1))
    load_f.wait()

    pl.semaphore_wait(barrier, 61 + 23)

    pending = []

    def cut(d, first, size, width):
        if d == 0:
            return first, first, size
        if d > 0:
            return first + size - width, first - width, width
        return first, first + size, width

    def send_near(slot, ref, blocks, rows, block_width, row_width):
        copies = []
        for n, (dg, dq) in enumerate(near):
            bs, bt, bn = cut(dg, blocks[0], blocks[1], block_width)
            rs, rt, rn = cut(dq, rows[0], rows[1], row_width)
            copy = pltpu.make_async_remote_copy(
                src_ref=ref.at[pl.ds(bs, bn), pl.ds(rs, rn)],
                dst_ref=ref.at[pl.ds(bt, bn), pl.ds(rt, rn)],
                send_sem=send_sem.at[slot, n],
                recv_sem=near_recv.at[slot, n],
                device_id=device(dg, dq),
                device_id_type=MESH,
            )
            copy.start()
            copies.append(copy)
        pending.extend(copies)
        return copies

    def arrive(copies):
        for copy in copies:
            copy.wait_recv()

    b0_copies = send_near(0, l0.b, (3, 16), (O0, 32), 3, 3)
    f0_copies = send_near(1, l0.f, (3, 16), (O0, 32), 2, 2)
    b1_copies = send_near(2, l1.b, (3, 4), (O1, 16), 2, 4)

    def clear(ref, blocks, rows, total_blocks, block_width, row_width):
        first, count = blocks
        start, height = rows

        @pl.when(g == 0)
        def _():
            for i in range(first - block_width, first):
                ref[i] = jnp.zeros(ref.shape[1:], F32)

        @pl.when(g == NG - 1)
        def _():
            for i in range(first + count, first + count + block_width):
                ref[i] = jnp.zeros(ref.shape[1:], F32)

        @pl.when(q == 0)
        def _():
            for i in range(first - block_width, first + count + block_width):
                ref[i, pl.ds(start - row_width, row_width), :] = jnp.zeros((row_width, 128), F32)

        @pl.when(q == NQ - 1)
        def _():
            for i in range(first - block_width, first + count + block_width):
                ref[i, pl.ds(start + height, row_width), :] = jnp.zeros((row_width, 128), F32)

    arrive(b0_copies)
    clear(l0.b, (3, 16), (O0, 32), 22, 3, 3)
    each(1, 21, l0.weigh, 2)
    arrive(f0_copies)
    each(1, 21, l0.first, 4)
    each(2, 20, lambda i: l0.store(l0.u, i, l0.smooth(l0.v, i)), 2)

    def store_f1(i, v):
        l1.f[3 + i, pl.ds(O1, 16), :] = v

    each(0, 4, restrict_0(lambda p: l0.residual(3 + p)[O0 - 8 : O0 - 8 + 32], store_f1))
    f1_copies = send_near(3, l1.f, (3, 4), (O1, 16), 2, 4)

    arrive(b1_copies)
    clear(l1.b, (3, 4), (O1, 16), 10, 2, 4)
    b2_own[pl.ds(7, 10), :] = restrict_1(lambda i: l1.b[3 + i, pl.ds(O1 - 2, 20), :], 10)

    def send_wide(slot, parts):
        copies = []
        for n, (dg, dq) in enumerate(wide):
            src, dst = parts(dq)
            copy = pltpu.make_async_remote_copy(
                src_ref=src,
                dst_ref=dst,
                send_sem=send_sem.at[4 + slot, n],
                recv_sem=wide_recv.at[slot, n],
                device_id=device(dg, dq),
                device_id_type=MESH,
            )
            copy.start()
            copies.append(copy)
        pending.extend(copies)
        return copies

    def b2_parts(dq):
        src, dst, n = {0: (8, O2, 8), 1: (7, O2 - 9, 9), -1: (8, O2 + 8, 9)}[dq]
        return b2_own.at[pl.ds(src, n)], l2.b.at[1 + g, pl.ds(dst, n)]

    b2_copies = send_wide(0, b2_parts)
    l2.b[1 + g, pl.ds(O2, 8), :] = b2_own[pl.ds(8, 8), :]
    each(1, 9, l1.weigh)
    arrive(f1_copies)
    each(1, 9, l1.first)
    each(2, 8, lambda i: l1.store(l1.u, i, l1.smooth(l1.v, i)))
    f2_own[...] = restrict_1(lambda i: l1.residual(3 + i)[O1 - 8 : O1 - 8 + 16], 8)

    def f2_parts(dq):
        return f2_own, l2.f.at[1 + g, pl.ds(O2 - 8 * dq, 8)]

    f2_copies = send_wide(1, f2_parts)
    l2.f[1 + g, pl.ds(O2, 8), :] = f2_own[...]

    arrive(b2_copies)

    @pl.when(q == 0)
    def _():
        for i in range(1, 9):
            l2.b[i, pl.ds(O2 - 9, 9), :] = jnp.zeros((9, 128), F32)

    @pl.when(q == NQ - 1)
    def _():
        for i in range(1, 9):
            l2.b[i, pl.ds(O2 + 8, 9), :] = jnp.zeros((9, 128), F32)

    each(1, 9, l2.weigh)
    b3_of = restrict_2(lambda i: l2.load(l2.b, i))

    def store_b3(i):
        l3.b[i, pl.ds(O3 - 4, 12), :] = b3_of(i)

    each(1, 9, store_b3)
    each(1, 9, l3.weigh)
    b4 = restrict_3(lambda i: l3.b[1 + i, pl.ds(O3, 4), :])

    arrive(f2_copies)
    each(1, 9, l2.first)
    each(1, 9, lambda i: l2.store(l2.u, i, l2.smooth(l2.v, i)))
    f3_of = restrict_2(l2.residual)

    def store_f3(i):
        l3.f[i, pl.ds(O3 - 4, 12), :] = f3_of(i)

    each(1, 9, store_f3)
    each(1, 9, l3.first)
    each(1, 9, lambda i: l3.store(l3.u, i, l3.smooth(l3.v, i)))
    f4 = restrict_3(lambda i: l3.residual(1 + i)[O3 - 8 : O3 - 8 + 4])

    gathered[pl.ds(2 * q, 1), :] = f4
    gathered[pl.ds(2 * q + 1, 1), :] = b4
    far_copies = []
    for n, d in enumerate(far):
        here = gathered.at[pl.ds(2 * q, 2)]
        copy = pltpu.make_async_remote_copy(
            src_ref=here,
            dst_ref=here,
            send_sem=send_sem.at[6, n],
            recv_sem=far_recv.at[n],
            device_id=device(0, d),
            device_id_type=MESH,
        )
        copy.start()
        far_copies.append(copy)
    pending.extend(far_copies)
    arrive(far_copies)

    source = gathered[pl.ds(0, NQ, stride=2), :]
    weight = gathered[pl.ds(1, NQ, stride=2), :]
    lane = lanes_of(NQ)
    row = lax.broadcasted_iota(jnp.int32, (NQ, 128), 0)
    odd = (lane & 1) == 1
    plane = (lane // 2) & 7
    edges = (
        plane == 7,
        plane == 0,
        (row == NQ - 1) & odd,
        (row == 0) & jnp.logical_not(odd),
        lane >= 112,
        lane < 16,
    )

    def bottom_shifts(v):
        up, down = roll(v, -1), roll(v, 1)
        yp = jnp.where(odd, pltpu.roll(down, NQ - 1, 0), up)
        ym = jnp.where(odd, down, pltpu.roll(up, 1, 0))
        return roll(v, -2), roll(v, 2), yp, ym, roll(v, -16), roll(v, 16)

    half = 0.5 * 0.25**4
    bottom_w = []
    bottom_d = None
    for edge, other in zip(edges, bottom_shifts(weight)):
        w = half * (weight + jnp.where(edge, 0.0, other))
        bottom_d = w if bottom_d is None else bottom_d + w
        bottom_w.append(jnp.where(edge, 0.0, w))

    def apply_op(v):
        result = bottom_d * v
        for w, other in zip(bottom_w, bottom_shifts(v)):
            result = result - w * other
        return result

    def total(v):
        return jnp.sum(v, keepdims=True)

    answer = None
    residual = source
    direction = source
    applied = None
    rho = total(source * source)
    rho_prev = rho
    alpha = omega = None
    for turn in range(BITERS):
        if turn > 0:
            beta = (rho / rho_prev) * (alpha / omega)
            direction = residual + beta * (direction - omega * applied)
        applied = apply_op(direction)
        alpha = rho / total(source * applied)
        middle = residual - alpha * applied
        bent = apply_op(middle)
        omega = total(bent * middle) / total(bent * bent)
        step = alpha * direction + omega * middle
        answer = step if answer is None else answer + step
        residual = middle - omega * bent
        if turn + 1 < BITERS:
            rho_prev = rho
            rho = total(source * residual)

    e_pad[pl.ds(8, NQ), :] = answer
    fine = lax.broadcasted_iota(jnp.int32, (16, 128), 0) - 8
    near_rows = jnp.where(
        fine < 0,
        e_pad[pl.ds(7 + q, 1), :],
        jnp.where(fine < 4, e_pad[pl.ds(8 + q, 1), :], e_pad[pl.ds(9 + q, 1), :]),
    )
    parity = jnp.where((fine < 0) | ((fine >= 2) & (fine < 4)), 1, 0)
    group = lanes_of(16) & ~15

    def pick(v, index):
        return jnp.take_along_axis(v, index, axis=1)

    def up_3(i):
        wide_e = pick(near_rows, group + parity + 2 * (i - 1))
        l3.store(l3.v, i, l3.load(l3.u, i) + wide_e)

    each(1, 9, up_3)

    def up_3s(i):
        v = l3.smooth(l3.v, i)
        v = v[6:14]
        for k in range(2):
            pair[i, pl.ds(k, 8, stride=2), :] = v
        mid = l2.u[i, pl.ds(O2 - 4, 16), :] + pair[i, pl.ds(0, 16), :]
        l2.v[i, pl.ds(O2 - 4, 16), :] = mid

    each(1, 9, up_3s)
    each(1, 9, lambda i: l2.store(l2.u, i, l2.smooth(l2.v, i)))

    spread = lanes_of(12) & ~3
    for i in range(-1, 5):
        from_block = 1 + g + (i // 4)
        v = pick(l2.u[from_block, pl.ds(O2 - 2, 12), :], spread + (i % 4))
        for k in range(2):
            pair[i + 1, pl.ds(k, 12, stride=2), :] = v
        l1.v[3 + i, pl.ds(O1 - 4, 24), :] = l1.u[3 + i, pl.ds(O1 - 4, 24), :] + pair[i + 1, pl.ds(0, 24), :]
    for i in range(-1, 5):
        l1.store(l1.u, 3 + i, l1.smooth(l1.v, 3 + i))

    even20 = (lanes_of(20) & 1) == 0
    for i in range(-1, 9):
        v = l1.u[3 + (i // 2), pl.ds(O1 - 2, 20), :]
        v = jnp.where(even20, v, roll(v, 1)) if i % 2 == 0 else jnp.where(even20, roll(v, -1), v)
        for k in range(2):
            pair[i + 1, pl.ds(k, 20, stride=2), :] = v
        wide_v = pair[i + 1, pl.ds(0, 40), :]
        for p in (2 * i, 2 * i + 1):
            if -1 <= p <= 16:
                l0.store(l0.v, 3 + p, l0.load(l0.u, 3 + p) + wide_v)

    def finish(p):
        out[p] = l0.smooth(l0.v, 3 + p)[O0 - 8 : O0 - 8 + 32]

    each(0, 16, finish, 2)

    for copy in pending:
        copy.wait_send()


def per_device(right_side, coefficient):
    scratch = []
    for blocks, rows in LEVEL_SHAPES:
        scratch += [pltpu.VMEM((blocks, rows, 128), F32)] * 6
        scratch.append(pltpu.VMEM((6, blocks, rows, 128), F32))
    scratch += [
        pltpu.VMEM((16, 48, 128), F32),
        pltpu.VMEM((24, 128), F32),
        pltpu.VMEM((8, 128), F32),
        pltpu.VMEM((2 * NQ, 128), F32),
        pltpu.VMEM((80, 128), F32),
        pltpu.SemaphoreType.DMA((2,)),
        pltpu.SemaphoreType.DMA((7, 64)),
        pltpu.SemaphoreType.DMA((4, 8)),
        pltpu.SemaphoreType.DMA((2, 23)),
        pltpu.SemaphoreType.DMA((63,)),
    ]
    return pl.pallas_call(
        kernel,
        out_shape=jax.ShapeDtypeStruct((16, 32, 128), F32),
        in_specs=[pl.BlockSpec(memory_space=pl.ANY)] * 2,
        out_specs=pl.BlockSpec(memory_space=pltpu.VMEM),
        scratch_shapes=scratch,
        compiler_params=pltpu.CompilerParams(
            collective_id=0, has_side_effects=True, vmem_limit_bytes=40 * 2**20
        ),
        cost_estimate=pl.CostEstimate(flops=10_000_000, bytes_accessed=3 * 262144, transcendentals=0),
    )(right_side, coefficient)


def solution(mesh):
    return jax.shard_map(
        per_device,
        mesh=mesh,
        in_specs=(P("gx", "yz", None), P("gx", "yz", None)),
        out_specs=P("gx", "yz", None),
        check_vma=False,
    )
```

```python
import jax
import jax.numpy as jnp
from jax import lax
from jax.experimental import pallas as pl
from jax.experimental.pallas import tpu as pltpu
from jax.sharding import PartitionSpec as P

MESH = pl.DeviceIdType.MESH
BITERS = 4
OMEGA = 0.8
NG = 8
NQ = 64
F32 = jnp.float32


def roll(v, by):
    return pltpu.roll(v, by % 128, 1)


def lanes_of(rows):
    return lax.broadcasted_iota(jnp.int32, (rows, 128), 1)


def swap(v, bit):
    lane = lanes_of(v.shape[0])
    return jnp.where((lane & bit) == 0, roll(v, -bit), roll(v, bit))


class Level:
    def __init__(self, scale, rows, start, count, unit, planes, depth, pieces):
        self.half = 0.5 * scale
        self.rows = rows
        self.start = start
        self.unit = unit
        self.planes = planes
        self.depth = depth

    def load(self, ref, i, shift=0):
        return ref[i, pl.ds(self.start + shift, self.rows), :]

    def store(self, ref, i, v):
        ref[i, pl.ds(self.start, self.rows), :] = v

    def shifted(self, ref, i):
        c = self.load(ref, i)
        if self.planes == 1:
            xp, xm = self.load(ref, i + 1), self.load(ref, i - 1)
        else:
            n, s = self.planes, self.unit
            field = (lanes_of(self.rows) // s) & (n - 1)
            xp = jnp.where(field < n - 1, roll(c, -s), roll(self.load(ref, i + 1), (n - 1) * s))
            xm = jnp.where(field > 0, roll(c, s), roll(self.load(ref, i - 1), -(n - 1) * s))
        yp, ym = self.load(ref, i, 1), self.load(ref, i, -1)
        zp, zm = roll(c, -self.depth), roll(c, self.depth)
        return c, (xp, xm, yp, ym, zp, zm)

    def weigh(self, i):
        lane = lanes_of(self.rows)
        first, last = lane < self.depth, lane >= 128 - self.depth
        c, others = self.shifted(self.b, i)
        total = None
        for k, other in enumerate(others):
            edge = {4: last, 5: first}.get(k)
            if edge is not None:
                other = jnp.where(edge, 0.0, other)
            w = self.half * (c + other)
            total = w if total is None else total + w
            if edge is not None:
                w = jnp.where(edge, 0.0, w)
            self.w[k, i, pl.ds(self.start, self.rows), :] = w
        self.store(self.d, i, total)
        inside = c > 0.0
        self.store(self.inv, i, jnp.where(inside, OMEGA / jnp.where(inside, total, 1.0), 0.0))

    def first(self, i):
        self.store(self.v, i, self.load(self.inv, i) * self.load(self.f, i))

    def around(self, ref, i):
        c, others = self.shifted(ref, i)
        total = None
        for k, other in enumerate(others):
            term = self.w[k, i, pl.ds(self.start, self.rows), :] * other
            total = term if total is None else total + term
        return c, total

    def smooth(self, src, i):
        c, s = self.around(src, i)
        return (1.0 - OMEGA) * c + self.load(self.inv, i) * (self.load(self.f, i) + s)

    def residual(self, i):
        c, s = self.around(self.u, i)
        return self.load(self.f, i) + s - self.load(self.d, i) * c


def each(lo, hi, body, group=None):
    if group is None:
        for i in range(lo, hi):
            body(i)
    else:
        assert (hi - lo) % group == 0

        def step(t, carry):
            for k in range(group):
                body(lo + t * group + k)
            return carry

        lax.fori_loop(0, (hi - lo) // group, step, 0)


R0, O0 = 56, 12
R1, O1 = 40, 12
R2, O2 = 40, 16
R3, O3 = 32, 16

LEVEL_SHAPES = ((22, R0), (10, R1), (10, R2), (10, R3))

GROUP_ROWS = ((6, 54), (13, 16), (16, 8), (16, 8), (5, 40), (4, 46), (3, 42))


def kernel(f_hbm, b_hbm, out, *refs):
    refs = list(refs)

    def take(n):
        got = refs[:n]
        del refs[:n]
        return got

    lv = [
        Level(1.0, 40, 8, 16, 1, 1, 1, 1),
        Level(0.25, 24, 8, 4, 1, 2, 2, 1),
        Level(0.0625, 24, 8, 8, 1, 4, 4, 1),
        Level(0.015625, 16, 8, 8, 2, 2, 8, 1),
    ]
    for one in lv:
        one.b, one.f, one.v, one.u, one.d, one.inv, one.w = take(7)
    pair, b2_own, f2_own, gathered, e_pad = take(5)
    load_sem, send_sem, recv_sem = take(3)
    l0, l1, l2, l3 = lv

    g, q = lax.axis_index("gx"), lax.axis_index("yz")

    load_b = pltpu.make_async_copy(b_hbm, l0.b.at[pl.ds(3, 16), pl.ds(O0, 32)], load_sem.at[0])
    load_f = pltpu.make_async_copy(f_hbm, l0.f.at[pl.ds(3, 16), pl.ds(O0, 32)], load_sem.at[1])
    load_b.start()
    load_f.start()

    def device(dg, dq):
        return {"gx": lax.rem(g + dg + NG, NG), "yz": lax.rem(q + dq + NQ, NQ)}

    near = [(dg, dq) for dg in (-1, 0, 1) for dq in (-1, 0, 1) if dg or dq]
    wide = [(dg, dq) for dg in (4, 3, 5, 2, 6, 1, 7, 0) for dq in (-1, 1, 0) if dg or dq]

    def yz_order():
        order = []
        for d in range(1, NQ):
            z, x = d % 16, d // 16
            order.append((-(min(z, 16 - z) + min(x, 4 - x)), d))
        return [d for _, d in sorted(order)]

    far = yz_order()

    barrier = pltpu.get_barrier_semaphore()

    def greet(target):
        pl.semaphore_signal(barrier, inc=1, device_id=target, device_id_type=MESH)

    for d in far:
        if d not in (1, NQ - 1):
            greet(device(0, d))
    for dg, dq in wide:
        greet(device(dg, dq))

    for one, (blocks, rows) in ((l1, LEVEL_SHAPES[1]), (l2, LEVEL_SHAPES[2]), (l3, LEVEL_SHAPES[3])):
        for ref in (one.b, one.v, one.u):
            for i in (0, blocks - 1):
                ref[i] = jnp.zeros((rows, 128), F32)
    for ref in (l3.b, l3.f):
        for i in range(1, 9):
            ref[i] = jnp.zeros((R3, 128), F32)
    e_pad[pl.ds(0, 8), :] = jnp.zeros((8, 128), F32)
    e_pad[pl.ds(72, 8), :] = jnp.zeros((8, 128), F32)

    even = (lanes_of(16) & 1) == 0

    def restrict_0(make, store):
        def body(i):
            halves = []
            for half in range(2):
                slot = 2 * i + half
                pair[slot, pl.ds(0, 32), :] = make(2 * slot) + make(2 * slot + 1)
                t = pair[slot, pl.ds(0, 16, stride=2), :] + pair[slot, pl.ds(1, 16, stride=2), :]
                halves.append(t + swap(t, 1))
            store(i, 0.125 * jnp.where(even, halves[0], halves[1]))

        return body

    def restrict_1(make, rows):
        lane = lanes_of(rows)
        packed = None
        for i in range(4):
            pair[i, pl.ds(0, 2 * rows), :] = make(i)
            t = pair[i, pl.ds(0, rows, stride=2), :] + pair[i, pl.ds(1, rows, stride=2), :]
            t = t + swap(t, 1)
            t = t + swap(t, 2)
            packed = t if packed is None else jnp.where((lane & 3) == i, t, packed)
        return 0.125 * packed

    def restrict_2(make):
        def one(i):
            pair[i, pl.ds(0, 24), :] = make(i)
            t = pair[i, pl.ds(0, 12, stride=2), :] + pair[i, pl.ds(1, 12, stride=2), :]
            t = t + swap(t, 1)
            return 0.125 * (t + swap(t, 4))

        return one

    def restrict_3(make):
        k = lanes_of(1) & 15
        row = None
        for i in range(8):
            pair[i, pl.ds(0, 4), :] = make(i)
            t = pair[i, pl.ds(0, 2, stride=2), :] + pair[i, pl.ds(1, 2, stride=2), :]
            t = t + swap(t, 2)
            t = 0.125 * (t + swap(t, 8))
            for j in range(2):
                row = t[j : j + 1] if row is None else jnp.where(k == 2 * i + j, t[j : j + 1], row)
        return row

    load_b.wait()

    def store_b1(i, v):
        l1.b[3 + i, pl.ds(O1, 16), :] = v

    each(0, 4, restrict_0(lambda p: l0.b[3 + p, pl.ds(O0, 32), :], store_b1))
    load_f.wait()

    pl.semaphore_wait(barrier, 61 + 23)

    def cut(d, first, size, width):
        if d == 0:
            return first, first, size
        if d > 0:
            return first + size - width, first - width, width
        return first, first + size, width

    def send_near(slot, ref, blocks, rows, block_width, row_width):
        for dg, dq in near:
            bs, bt, bn = cut(dg, blocks[0], blocks[1], block_width)
            rs, rt, rn = cut(dq, rows[0], rows[1], row_width)
            copy = pltpu.make_async_remote_copy(
                src_ref=ref.at[pl.ds(bs, bn), pl.ds(rs, rn)],
                dst_ref=ref.at[pl.ds(bt, bn), pl.ds(rt, rn)],
                send_sem=send_sem.at[slot],
                recv_sem=recv_sem.at[slot],
                device_id=device(dg, dq),
                device_id_type=MESH,
            )
            copy.start()

    def all_of(sem, shape):
        some = l0.w.at[(0,) + tuple(pl.ds(0, n) for n in shape)]
        return pltpu.make_async_copy(some, some, sem)

    def arrive(group):
        all_of(recv_sem.at[group], GROUP_ROWS[group]).wait()

    send_near(0, l0.b, (3, 16), (O0, 32), 3, 3)
    send_near(1, l0.f, (3, 16), (O0, 32), 2, 2)
    send_near(2, l1.b, (3, 4), (O1, 16), 2, 4)

    def clear(ref, blocks, rows, total_blocks, block_width, row_width):
        first, count = blocks
        start, height = rows

        @pl.when(g == 0)
        def _():
            for i in range(first - block_width, first):
                ref[i] = jnp.zeros(ref.shape[1:], F32)

        @pl.when(g == NG - 1)
        def _():
            for i in range(first + count, first + count + block_width):
                ref[i] = jnp.zeros(ref.shape[1:], F32)

        @pl.when(q == 0)
        def _():
            for i in range(first - block_width, first + count + block_width):
                ref[i, pl.ds(start - row_width, row_width), :] = jnp.zeros((row_width, 128), F32)

        @pl.when(q == NQ - 1)
        def _():
            for i in range(first - block_width, first + count + block_width):
                ref[i, pl.ds(start + height, row_width), :] = jnp.zeros((row_width, 128), F32)

    arrive(0)
    clear(l0.b, (3, 16), (O0, 32), 22, 3, 3)
    each(1, 21, l0.weigh, 10)
    arrive(1)
    each(1, 21, l0.first, 10)
    each(2, 20, lambda i: l0.store(l0.u, i, l0.smooth(l0.v, i)), 9)

    def store_f1(i, v):
        l1.f[3 + i, pl.ds(O1, 16), :] = v

    each(0, 4, restrict_0(lambda p: l0.residual(3 + p)[O0 - 8 : O0 - 8 + 32], store_f1))
    send_near(3, l1.f, (3, 4), (O1, 16), 2, 4)

    arrive(2)
    clear(l1.b, (3, 4), (O1, 16), 10, 2, 4)
    b2_own[pl.ds(7, 10), :] = restrict_1(lambda i: l1.b[3 + i, pl.ds(O1 - 2, 20), :], 10)

    def send_wide(slot, parts):
        for dg, dq in wide:
            src, dst = parts(dq)
            copy = pltpu.make_async_remote_copy(
                src_ref=src,
                dst_ref=dst,
                send_sem=send_sem.at[slot],
                recv_sem=recv_sem.at[slot],
                device_id=device(dg, dq),
                device_id_type=MESH,
            )
            copy.start()

    def b2_parts(dq):
        src, dst, n = {0: (8, O2, 8), 1: (7, O2 - 9, 9), -1: (8, O2 + 8, 9)}[dq]
        return b2_own.at[pl.ds(src, n)], l2.b.at[1 + g, pl.ds(dst, n)]

    send_wide(4, b2_parts)
    l2.b[1 + g, pl.ds(O2, 8), :] = b2_own[pl.ds(8, 8), :]
    each(1, 9, l1.weigh)
    arrive(3)
    each(1, 9, l1.first)
    each(2, 8, lambda i: l1.store(l1.u, i, l1.smooth(l1.v, i)))
    f2_own[...] = restrict_1(lambda i: l1.residual(3 + i)[O1 - 8 : O1 - 8 + 16], 8)

    def f2_parts(dq):
        return f2_own, l2.f.at[1 + g, pl.ds(O2 - 8 * dq, 8)]

    send_wide(5, f2_parts)
    l2.f[1 + g, pl.ds(O2, 8), :] = f2_own[...]

    arrive(4)

    @pl.when(q == 0)
    def _():
        for i in range(1, 9):
            l2.b[i, pl.ds(O2 - 9, 9), :] = jnp.zeros((9, 128), F32)

    @pl.when(q == NQ - 1)
    def _():
        for i in range(1, 9):
            l2.b[i, pl.ds(O2 + 8, 9), :] = jnp.zeros((9, 128), F32)

    each(1, 9, l2.weigh)
    b3_of = restrict_2(lambda i: l2.load(l2.b, i))

    def store_b3(i):
        l3.b[i, pl.ds(O3 - 4, 12), :] = b3_of(i)

    each(1, 9, store_b3)
    each(1, 9, l3.weigh)
    b4 = restrict_3(lambda i: l3.b[1 + i, pl.ds(O3, 4), :])

    arrive(5)
    each(1, 9, l2.first)
    each(1, 9, lambda i: l2.store(l2.u, i, l2.smooth(l2.v, i)))
    f3_of = restrict_2(l2.residual)

    def store_f3(i):
        l3.f[i, pl.ds(O3 - 4, 12), :] = f3_of(i)

    each(1, 9, store_f3)
    each(1, 9, l3.first)
    each(1, 9, lambda i: l3.store(l3.u, i, l3.smooth(l3.v, i)))
    f4 = restrict_3(lambda i: l3.residual(1 + i)[O3 - 8 : O3 - 8 + 4])

    gathered[pl.ds(2 * q, 1), :] = f4
    gathered[pl.ds(2 * q + 1, 1), :] = b4
    for d in far:
        here = gathered.at[pl.ds(2 * q, 2)]
        copy = pltpu.make_async_remote_copy(
            src_ref=here,
            dst_ref=here,
            send_sem=send_sem.at[6],
            recv_sem=recv_sem.at[6],
            device_id=device(0, d),
            device_id_type=MESH,
        )
        copy.start()
    arrive(6)

    source = gathered[pl.ds(0, NQ, stride=2), :]
    weight = gathered[pl.ds(1, NQ, stride=2), :]
    lane = lanes_of(NQ)
    row = lax.broadcasted_iota(jnp.int32, (NQ, 128), 0)
    odd = (lane & 1) == 1
    plane = (lane // 2) & 7
    edges = (
        plane == 7,
        plane == 0,
        (row == NQ - 1) & odd,
        (row == 0) & jnp.logical_not(odd),
        lane >= 112,
        lane < 16,
    )

    def bottom_shifts(v):
        up, down = roll(v, -1), roll(v, 1)
        yp = jnp.where(odd, pltpu.roll(down, NQ - 1, 0), up)
        ym = jnp.where(odd, down, pltpu.roll(up, 1, 0))
        return roll(v, -2), roll(v, 2), yp, ym, roll(v, -16), roll(v, 16)

    half = 0.5 * 0.25**4
    bottom_w = []
    bottom_d = None
    for edge, other in zip(edges, bottom_shifts(weight)):
        w = half * (weight + jnp.where(edge, 0.0, other))
        bottom_d = w if bottom_d is None else bottom_d + w
        bottom_w.append(jnp.where(edge, 0.0, w))

    def apply_op(v):
        result = bottom_d * v
        for w, other in zip(bottom_w, bottom_shifts(v)):
            result = result - w * other
        return result

    def total(v):
        return jnp.sum(v, keepdims=True)

    answer = None
    residual = source
    direction = source
    applied = None
    rho = total(source * source)
    rho_prev = rho
    alpha = omega = None
    for turn in range(BITERS):
        if turn > 0:
            beta = (rho / rho_prev) * (alpha / omega)
            direction = residual + beta * (direction - omega * applied)
        applied = apply_op(direction)
        alpha = rho / total(source * applied)
        middle = residual - alpha * applied
        bent = apply_op(middle)
        omega = total(bent * middle) / total(bent * bent)
        step = alpha * direction + omega * middle
        answer = step if answer is None else answer + step
        residual = middle - omega * bent
        if turn + 1 < BITERS:
            rho_prev = rho
            rho = total(source * residual)

    e_pad[pl.ds(8, NQ), :] = answer
    fine = lax.broadcasted_iota(jnp.int32, (16, 128), 0) - 8
    near_rows = jnp.where(
        fine < 0,
        e_pad[pl.ds(7 + q, 1), :],
        jnp.where(fine < 4, e_pad[pl.ds(8 + q, 1), :], e_pad[pl.ds(9 + q, 1), :]),
    )
    parity = jnp.where((fine < 0) | ((fine >= 2) & (fine < 4)), 1, 0)
    group = lanes_of(16) & ~15

    def pick(v, index):
        return jnp.take_along_axis(v, index, axis=1)

    def up_3(i):
        wide_e = pick(near_rows, group + parity + 2 * (i - 1))
        l3.store(l3.v, i, l3.load(l3.u, i) + wide_e)

    each(1, 9, up_3)

    def up_3s(i):
        v = l3.smooth(l3.v, i)
        v = v[6:14]
        for k in range(2):
            pair[i, pl.ds(k, 8, stride=2), :] = v
        mid = l2.u[i, pl.ds(O2 - 4, 16), :] + pair[i, pl.ds(0, 16), :]
        l2.v[i, pl.ds(O2 - 4, 16), :] = mid

    each(1, 9, up_3s)
    each(1, 9, lambda i: l2.store(l2.u, i, l2.smooth(l2.v, i)))

    spread = lanes_of(12) & ~3
    for i in range(-1, 5):
        from_block = 1 + g + (i // 4)
        v = pick(l2.u[from_block, pl.ds(O2 - 2, 12), :], spread + (i % 4))
        for k in range(2):
            pair[i + 1, pl.ds(k, 12, stride=2), :] = v
        l1.v[3 + i, pl.ds(O1 - 4, 24), :] = l1.u[3 + i, pl.ds(O1 - 4, 24), :] + pair[i + 1, pl.ds(0, 24), :]
    for i in range(-1, 5):
        l1.store(l1.u, 3 + i, l1.smooth(l1.v, 3 + i))

    even20 = (lanes_of(20) & 1) == 0
    for i in range(-1, 9):
        v = l1.u[3 + (i // 2), pl.ds(O1 - 2, 20), :]
        v = jnp.where(even20, v, roll(v, 1)) if i % 2 == 0 else jnp.where(even20, roll(v, -1), v)
        for k in range(2):
            pair[i + 1, pl.ds(k, 20, stride=2), :] = v
        wide_v = pair[i + 1, pl.ds(0, 40), :]
        for p in (2 * i, 2 * i + 1):
            if -1 <= p <= 16:
                l0.store(l0.v, 3 + p, l0.load(l0.u, 3 + p) + wide_v)

    def finish(p):
        out[p] = l0.smooth(l0.v, 3 + p)[O0 - 8 : O0 - 8 + 32]

    each(0, 16, finish, 8)

    for group, shape in enumerate(GROUP_ROWS):
        all_of(send_sem.at[group], shape).wait()


def per_device(right_side, coefficient):
    scratch = []
    for blocks, rows in LEVEL_SHAPES:
        scratch += [pltpu.VMEM((blocks, rows, 128), F32)] * 6
        scratch.append(pltpu.VMEM((6, blocks, rows, 128), F32))
    scratch += [
        pltpu.VMEM((16, 48, 128), F32),
        pltpu.VMEM((24, 128), F32),
        pltpu.VMEM((8, 128), F32),
        pltpu.VMEM((2 * NQ, 128), F32),
        pltpu.VMEM((80, 128), F32),
        pltpu.SemaphoreType.DMA((2,)),
        pltpu.SemaphoreType.DMA((7,)),
        pltpu.SemaphoreType.DMA((7,)),
    ]
    return pl.pallas_call(
        kernel,
        out_shape=jax.ShapeDtypeStruct((16, 32, 128), F32),
        in_specs=[pl.BlockSpec(memory_space=pltpu.HBM)] * 2,
        out_specs=pl.BlockSpec(memory_space=pltpu.VMEM),
        scratch_shapes=scratch,
        compiler_params=pltpu.CompilerParams(
            collective_id=0, has_side_effects=True, vmem_limit_bytes=60 * 2**20
        ),
        cost_estimate=pl.CostEstimate(flops=10_000_000, bytes_accessed=3 * 262144, transcendentals=0),
    )(right_side, coefficient)


def solution(mesh):
    return jax.shard_map(
        per_device,
        mesh=mesh,
        in_specs=(P("gx", "yz", None), P("gx", "yz", None)),
        out_specs=P("gx", "yz", None),
        check_vma=False,
    )
```

```python
import jax
import jax.numpy as jnp
from jax import lax
from jax.experimental import pallas as pl
from jax.experimental.pallas import tpu as pltpu
from jax.sharding import PartitionSpec as P

MESH = pl.DeviceIdType.MESH
BITERS = 4
OMEGA = 0.8
NG = 8
NQ = 64
F32 = jnp.float32


def roll(v, by):
    return pltpu.roll(v, by % 128, 1)


def lanes_of(rows):
    return lax.broadcasted_iota(jnp.int32, (rows, 128), 1)


def swap(v, bit):
    lane = lanes_of(v.shape[0])
    return jnp.where((lane & bit) == 0, roll(v, -bit), roll(v, bit))


class Level:
    def __init__(self, scale, rows, start, count, unit, planes, depth, pieces):
        self.half = 0.5 * scale
        self.rows = rows
        self.start = start
        self.unit = unit
        self.planes = planes
        self.depth = depth

    def load(self, ref, i, shift=0):
        return ref[i, pl.ds(self.start + shift, self.rows), :]

    def store(self, ref, i, v):
        ref[i, pl.ds(self.start, self.rows), :] = v

    def shifted(self, ref, i):
        c = self.load(ref, i)
        if self.planes == 1:
            xp, xm = self.load(ref, i + 1), self.load(ref, i - 1)
        else:
            s = self.unit
            bits = (self.planes - 1) * s
            field = lanes_of(self.rows) & bits
            xp = jnp.where(field != bits, roll(c, -s), roll(self.load(ref, i + 1), bits))
            xm = jnp.where(field != 0, roll(c, s), roll(self.load(ref, i - 1), -bits))
        yp, ym = self.load(ref, i, 1), self.load(ref, i, -1)
        zp, zm = roll(c, -self.depth), roll(c, self.depth)
        return c, (xp, xm, yp, ym, zp, zm)

    def weigh(self, i):
        lane = lanes_of(self.rows)
        first, last = lane < self.depth, lane >= 128 - self.depth
        c, others = self.shifted(self.b, i)
        total = None
        for k, other in enumerate(others):
            edge = {4: last, 5: first}.get(k)
            if edge is not None:
                other = jnp.where(edge, 0.0, other)
            w = self.half * (c + other)
            total = w if total is None else total + w
            if edge is not None:
                w = jnp.where(edge, 0.0, w)
            self.w[k, i, pl.ds(self.start, self.rows), :] = w
        self.store(self.d, i, total)
        inside = c > 0.0
        self.store(self.inv, i, jnp.where(inside, OMEGA / jnp.where(inside, total, 1.0), 0.0))

    def first(self, i):
        self.store(self.v, i, self.load(self.inv, i) * self.load(self.f, i))

    def around(self, ref, i):
        c, others = self.shifted(ref, i)
        total = None
        for k, other in enumerate(others):
            term = self.w[k, i, pl.ds(self.start, self.rows), :] * other
            total = term if total is None else total + term
        return c, total

    def smooth(self, src, i):
        c, s = self.around(src, i)
        return (1.0 - OMEGA) * c + self.load(self.inv, i) * (self.load(self.f, i) + s)

    def residual(self, i):
        c, s = self.around(self.u, i)
        return self.load(self.f, i) + s - self.load(self.d, i) * c


def each(lo, hi, body, group=None):
    if group is None:
        for i in range(lo, hi):
            body(i)
    else:
        assert (hi - lo) % group == 0

        def step(t, carry):
            for k in range(group):
                body(lo + t * group + k)
            return carry

        lax.fori_loop(0, (hi - lo) // group, step, 0)


R0, O0 = 56, 12
R1, O1 = 40, 12
R2, O2 = 40, 16
R3, O3 = 32, 16

LEVEL_SHAPES = ((22, R0), (10, R1), (10, R2), (10, R3))

GROUP_ROWS = ((6, 54), (13, 16), (16, 8), (16, 8), (5, 40), (4, 46), (3, 42))


def kernel(f_hbm, b_hbm, out, *refs):
    refs = list(refs)

    def take(n):
        got = refs[:n]
        del refs[:n]
        return got

    lv = [
        Level(1.0, 40, 8, 16, 1, 1, 1, 1),
        Level(0.25, 24, 8, 4, 1, 2, 2, 1),
        Level(0.0625, 24, 8, 8, 1, 4, 4, 1),
        Level(0.015625, 16, 8, 8, 2, 2, 8, 1),
    ]
    for one in lv:
        one.b, one.f, one.v, one.u, one.d, one.inv, one.w = take(7)
    pair, b2_own, f2_own, gathered, e_pad = take(5)
    load_sem, send_sem, recv_sem, ready = take(4)
    l0, l1, l2, l3 = lv

    g, q = lax.axis_index("gx"), lax.axis_index("yz")

    load_b = pltpu.make_async_copy(b_hbm, l0.b.at[pl.ds(3, 16), pl.ds(O0, 32)], load_sem.at[0])
    load_f = pltpu.make_async_copy(f_hbm, l0.f.at[pl.ds(3, 16), pl.ds(O0, 32)], load_sem.at[1])
    load_b.start()
    load_f.start()

    def device(dg, dq):
        return {"gx": lax.rem(g + dg + NG, NG), "yz": lax.rem(q + dq + NQ, NQ)}

    near = [(dg, dq) for dg in (-1, 1) for dq in (-1, 1)] + [(0, -1), (0, 1), (-1, 0), (1, 0)]
    wide = [(dg, dq) for dg in (4, 3, 5, 2, 6, 1, 7, 0) for dq in (-1, 1, 0) if dg or dq]

    def yz_order():
        order = []
        for d in range(1, NQ):
            z, x = d % 16, d // 16
            order.append((-(min(z, 16 - z) + min(x, 4 - x)), d))
        return [d for _, d in sorted(order)]

    far = yz_order()

    barrier = pltpu.get_barrier_semaphore()

    def greet(target):
        pl.semaphore_signal(barrier, inc=1, device_id=target, device_id_type=MESH)

    def device_xz(dx, dz):
        return {"gx": g, "yz": ((q >> 4) + dx & 3) * 16 + (q + dz & 15)}

    greeted = [device(dg, dq) for dg, dq in near]
    greeted += [device(dg, dq) for dg in (-2, 2) for dq in (-1, 0, 1)]
    greeted += [device_xz(0, dz) for dz in (1, -1, 2, -2, 3, -3)]
    greeted += [device_xz(dx, 0) for dx in (1, 2, 3)]
    for target in greeted:
        greet(target)

    for one, (blocks, rows) in ((l1, LEVEL_SHAPES[1]), (l2, LEVEL_SHAPES[2]), (l3, LEVEL_SHAPES[3])):
        for ref in (one.b, one.v, one.u):
            for i in (0, blocks - 1):
                ref[i] = jnp.zeros((rows, 128), F32)
    for ref in (l3.b, l3.f):
        for i in range(1, 9):
            ref[i] = jnp.zeros((R3, 128), F32)
    e_pad[pl.ds(0, 8), :] = jnp.zeros((8, 128), F32)
    e_pad[pl.ds(72, 8), :] = jnp.zeros((8, 128), F32)

    even = (lanes_of(16) & 1) == 0

    def restrict_0(make, store):
        def body(i):
            halves = []
            for half in range(2):
                slot = 2 * i + half
                pair[slot, pl.ds(0, 32), :] = make(2 * slot) + make(2 * slot + 1)
                t = pair[slot, pl.ds(0, 16, stride=2), :] + pair[slot, pl.ds(1, 16, stride=2), :]
                halves.append(t + swap(t, 1))
            store(i, 0.125 * jnp.where(even, halves[0], halves[1]))

        return body

    def restrict_1(make, rows):
        lane = lanes_of(rows)
        packed = None
        for i in range(4):
            pair[i, pl.ds(0, 2 * rows), :] = make(i)
            t = pair[i, pl.ds(0, rows, stride=2), :] + pair[i, pl.ds(1, rows, stride=2), :]
            t = t + swap(t, 1)
            t = t + swap(t, 2)
            packed = t if packed is None else jnp.where((lane & 3) == i, t, packed)
        return 0.125 * packed

    def restrict_2(make):
        def one(i):
            pair[i, pl.ds(0, 24), :] = make(i)
            t = pair[i, pl.ds(0, 12, stride=2), :] + pair[i, pl.ds(1, 12, stride=2), :]
            t = t + swap(t, 1)
            return 0.125 * (t + swap(t, 4))

        return one

    def restrict_3(make):
        k = lanes_of(1) & 15
        row = None
        for i in range(8):
            pair[i, pl.ds(0, 4), :] = make(i)
            t = pair[i, pl.ds(0, 2, stride=2), :] + pair[i, pl.ds(1, 2, stride=2), :]
            t = t + swap(t, 2)
            t = 0.125 * (t + swap(t, 8))
            for j in range(2):
                row = t[j : j + 1] if row is None else jnp.where(k == 2 * i + j, t[j : j + 1], row)
        return row

    load_b.wait()

    def store_b1(i, v):
        l1.b[3 + i, pl.ds(O1, 16), :] = v

    each(0, 4, restrict_0(lambda p: l0.b[3 + p, pl.ds(O0, 32), :], store_b1))
    load_f.wait()

    pl.semaphore_wait(barrier, len(greeted))

    def pass_on(n, targets):
        for target in targets:
            pl.semaphore_signal(ready.at[n], inc=1, device_id=target, device_id_type=MESH)


    def cut(d, first, size, width):
        if d == 0:
            return first, first, size
        if d > 0:
            return first + size - width, first - width, width
        return first, first + size, width

    def send_near(slot, ref, blocks, rows, block_width, row_width):
        for dg, dq in near:
            bs, bt, bn = cut(dg, blocks[0], blocks[1], block_width)
            rs, rt, rn = cut(dq, rows[0], rows[1], row_width)
            copy = pltpu.make_async_remote_copy(
                src_ref=ref.at[pl.ds(bs, bn), pl.ds(rs, rn)],
                dst_ref=ref.at[pl.ds(bt, bn), pl.ds(rt, rn)],
                send_sem=send_sem.at[slot],
                recv_sem=recv_sem.at[slot],
                device_id=device(dg, dq),
                device_id_type=MESH,
            )
            copy.start()

    def all_of(sem, shape):
        some = l0.w.at[(0,) + tuple(pl.ds(0, n) for n in shape)]
        return pltpu.make_async_copy(some, some, sem)

    def arrive(group):
        all_of(recv_sem.at[group], GROUP_ROWS[group]).wait()

    send_near(0, l0.b, (3, 16), (O0, 32), 3, 3)
    send_near(1, l0.f, (3, 16), (O0, 32), 2, 2)
    send_near(2, l1.b, (3, 4), (O1, 16), 2, 4)
    pass_on(
        0,
        [device(dg, dq) for dg in (-2, 2) for dq in (-1, 0, 1)]
        + [device_xz(0, dz) for dz in (3, -3)],
    )

    def clear(ref, blocks, rows, total_blocks, block_width, row_width):
        first, count = blocks
        start, height = rows

        @pl.when(g == 0)
        def _():
            for i in range(first - block_width, first):
                ref[i] = jnp.zeros(ref.shape[1:], F32)

        @pl.when(g == NG - 1)
        def _():
            for i in range(first + count, first + count + block_width):
                ref[i] = jnp.zeros(ref.shape[1:], F32)

        @pl.when(q == 0)
        def _():
            for i in range(first - block_width, first + count + block_width):
                ref[i, pl.ds(start - row_width, row_width), :] = jnp.zeros((row_width, 128), F32)

        @pl.when(q == NQ - 1)
        def _():
            for i in range(first - block_width, first + count + block_width):
                ref[i, pl.ds(start + height, row_width), :] = jnp.zeros((row_width, 128), F32)

    arrive(0)
    clear(l0.b, (3, 16), (O0, 32), 22, 3, 3)
    each(1, 21, l0.weigh, 10)
    arrive(1)
    each(1, 21, l0.first, 10)
    each(2, 20, lambda i: l0.store(l0.u, i, l0.smooth(l0.v, i)), 9)

    def store_f1(i, v):
        l1.f[3 + i, pl.ds(O1, 16), :] = v

    each(0, 4, restrict_0(lambda p: l0.residual(3 + p)[O0 - 8 : O0 - 8 + 32], store_f1))
    send_near(3, l1.f, (3, 4), (O1, 16), 2, 4)

    arrive(2)
    clear(l1.b, (3, 4), (O1, 16), 10, 2, 4)
    b2_own[pl.ds(7, 10), :] = restrict_1(lambda i: l1.b[3 + i, pl.ds(O1 - 2, 20), :], 10)

    def send_wide(slot, parts):
        for dg, dq in wide:
            src, dst = parts(dq)
            copy = pltpu.make_async_remote_copy(
                src_ref=src,
                dst_ref=dst,
                send_sem=send_sem.at[slot],
                recv_sem=recv_sem.at[slot],
                device_id=device(dg, dq),
                device_id_type=MESH,
            )
            copy.start()

    pl.semaphore_wait(ready.at[0], 8)

    def b2_parts(dq):
        src, dst, n = {0: (8, O2, 8), 1: (7, O2 - 9, 9), -1: (8, O2 + 8, 9)}[dq]
        return b2_own.at[pl.ds(src, n)], l2.b.at[1 + g, pl.ds(dst, n)]

    send_wide(4, b2_parts)
    pass_on(1, [device_xz(dx, dz) for dx in range(4) for dz in (3, -3)])
    l2.b[1 + g, pl.ds(O2, 8), :] = b2_own[pl.ds(8, 8), :]
    each(1, 9, l1.weigh)
    arrive(3)
    each(1, 9, l1.first)
    each(2, 8, lambda i: l1.store(l1.u, i, l1.smooth(l1.v, i)))
    f2_own[...] = restrict_1(lambda i: l1.residual(3 + i)[O1 - 8 : O1 - 8 + 16], 8)

    def f2_parts(dq):
        return f2_own, l2.f.at[1 + g, pl.ds(O2 - 8 * dq, 8)]

    send_wide(5, f2_parts)
    l2.f[1 + g, pl.ds(O2, 8), :] = f2_own[...]

    arrive(4)

    @pl.when(q == 0)
    def _():
        for i in range(1, 9):
            l2.b[i, pl.ds(O2 - 9, 9), :] = jnp.zeros((9, 128), F32)

    @pl.when(q == NQ - 1)
    def _():
        for i in range(1, 9):
            l2.b[i, pl.ds(O2 + 8, 9), :] = jnp.zeros((9, 128), F32)

    each(1, 9, l2.weigh)
    b3_of = restrict_2(lambda i: l2.load(l2.b, i))

    def store_b3(i):
        l3.b[i, pl.ds(O3 - 4, 12), :] = b3_of(i)

    each(1, 9, store_b3)
    each(1, 9, l3.weigh)
    b4 = restrict_3(lambda i: l3.b[1 + i, pl.ds(O3, 4), :])

    arrive(5)
    each(1, 9, l2.first)
    each(1, 9, lambda i: l2.store(l2.u, i, l2.smooth(l2.v, i)))
    f3_of = restrict_2(l2.residual)

    def store_f3(i):
        l3.f[i, pl.ds(O3 - 4, 12), :] = f3_of(i)

    each(1, 9, store_f3)
    each(1, 9, l3.first)
    each(1, 9, lambda i: l3.store(l3.u, i, l3.smooth(l3.v, i)))
    f4 = restrict_3(lambda i: l3.residual(1 + i)[O3 - 8 : O3 - 8 + 4])

    gathered[pl.ds(2 * q, 1), :] = f4
    gathered[pl.ds(2 * q + 1, 1), :] = b4
    pl.semaphore_wait(ready.at[1], 8)
    for d in far:
        here = gathered.at[pl.ds(2 * q, 2)]
        copy = pltpu.make_async_remote_copy(
            src_ref=here,
            dst_ref=here,
            send_sem=send_sem.at[6],
            recv_sem=recv_sem.at[6],
            device_id=device(0, d),
            device_id_type=MESH,
        )
        copy.start()
    arrive(6)

    source = gathered[pl.ds(0, NQ, stride=2), :]
    weight = gathered[pl.ds(1, NQ, stride=2), :]
    lane = lanes_of(NQ)
    row = lax.broadcasted_iota(jnp.int32, (NQ, 128), 0)
    odd = (lane & 1) == 1
    edges = (
        (lane & 14) == 14,
        (lane & 14) == 0,
        (row == NQ - 1) & odd,
        (row == 0) & jnp.logical_not(odd),
        lane >= 112,
        lane < 16,
    )

    def bottom_shifts(v):
        up, down = roll(v, -1), roll(v, 1)
        yp = jnp.where(odd, pltpu.roll(down, NQ - 1, 0), up)
        ym = jnp.where(odd, down, pltpu.roll(up, 1, 0))
        return roll(v, -2), roll(v, 2), yp, ym, roll(v, -16), roll(v, 16)

    half = 0.5 * 0.25**4
    bottom_w = []
    bottom_d = None
    for edge, other in zip(edges, bottom_shifts(weight)):
        w = half * (weight + jnp.where(edge, 0.0, other))
        bottom_d = w if bottom_d is None else bottom_d + w
        bottom_w.append(jnp.where(edge, 0.0, w))

    def apply_op(v):
        result = bottom_d * v
        for w, other in zip(bottom_w, bottom_shifts(v)):
            result = result - w * other
        return result

    def total(v):
        return jnp.sum(v, keepdims=True)

    answer = None
    residual = source
    direction = source
    applied = None
    rho = total(source * source)
    rho_prev = rho
    alpha = omega = None
    for turn in range(BITERS):
        if turn > 0:
            beta = (rho / rho_prev) * (alpha / omega)
            direction = residual + beta * (direction - omega * applied)
        applied = apply_op(direction)
        alpha = rho / total(source * applied)
        middle = residual - alpha * applied
        bent = apply_op(middle)
        omega = total(bent * middle) / total(bent * bent)
        step = alpha * direction + omega * middle
        answer = step if answer is None else answer + step
        residual = middle - omega * bent
        if turn + 1 < BITERS:
            rho_prev = rho
            rho = total(source * residual)

    e_pad[pl.ds(8, NQ), :] = answer
    fine = lax.broadcasted_iota(jnp.int32, (16, 128), 0) - 8
    near_rows = jnp.where(
        fine < 0,
        e_pad[pl.ds(7 + q, 1), :],
        jnp.where(fine < 4, e_pad[pl.ds(8 + q, 1), :], e_pad[pl.ds(9 + q, 1), :]),
    )
    parity = jnp.where((fine < 0) | ((fine >= 2) & (fine < 4)), 1, 0)
    group = lanes_of(16) & ~15

    def pick(v, index):
        return jnp.take_along_axis(v, index, axis=1)

    def up_3(i):
        wide_e = pick(near_rows, group + parity + 2 * (i - 1))
        l3.store(l3.v, i, l3.load(l3.u, i) + wide_e)

    each(1, 9, up_3)

    def up_3s(i):
        v = l3.smooth(l3.v, i)
        v = v[6:14]
        for k in range(2):
            pair[i, pl.ds(k, 8, stride=2), :] = v
        mid = l2.u[i, pl.ds(O2 - 4, 16), :] + pair[i, pl.ds(0, 16), :]
        l2.v[i, pl.ds(O2 - 4, 16), :] = mid

    each(1, 9, up_3s)
    each(1, 9, lambda i: l2.store(l2.u, i, l2.smooth(l2.v, i)))

    spread = lanes_of(12) & ~3
    for i in range(-1, 5):
        from_block = 1 + g + (i // 4)
        v = pick(l2.u[from_block, pl.ds(O2 - 2, 12), :], spread + (i % 4))
        for k in range(2):
            pair[i + 1, pl.ds(k, 12, stride=2), :] = v
        l1.v[3 + i, pl.ds(O1 - 4, 24), :] = l1.u[3 + i, pl.ds(O1 - 4, 24), :] + pair[i + 1, pl.ds(0, 24), :]
    for i in range(-1, 5):
        l1.store(l1.u, 3 + i, l1.smooth(l1.v, 3 + i))

    even20 = (lanes_of(20) & 1) == 0
    for i in range(-1, 9):
        v = l1.u[3 + (i // 2), pl.ds(O1 - 2, 20), :]
        v = jnp.where(even20, v, roll(v, 1)) if i % 2 == 0 else jnp.where(even20, roll(v, -1), v)
        for k in range(2):
            pair[i + 1, pl.ds(k, 20, stride=2), :] = v
        wide_v = pair[i + 1, pl.ds(0, 40), :]
        for p in (2 * i, 2 * i + 1):
            if -1 <= p <= 16:
                l0.store(l0.v, 3 + p, l0.load(l0.u, 3 + p) + wide_v)

    def finish(p):
        out[p] = l0.smooth(l0.v, 3 + p)[O0 - 8 : O0 - 8 + 32]

    each(0, 16, finish, 8)

    for group, shape in enumerate(GROUP_ROWS):
        all_of(send_sem.at[group], shape).wait()


def per_device(right_side, coefficient):
    scratch = []
    for blocks, rows in LEVEL_SHAPES:
        scratch += [pltpu.VMEM((blocks, rows, 128), F32)] * 6
        scratch.append(pltpu.VMEM((6, blocks, rows, 128), F32))
    scratch += [
        pltpu.VMEM((16, 48, 128), F32),
        pltpu.VMEM((24, 128), F32),
        pltpu.VMEM((8, 128), F32),
        pltpu.VMEM((2 * NQ, 128), F32),
        pltpu.VMEM((80, 128), F32),
        pltpu.SemaphoreType.DMA((2,)),
        pltpu.SemaphoreType.DMA((7,)),
        pltpu.SemaphoreType.DMA((7,)),
        pltpu.SemaphoreType.REGULAR((2,)),
    ]
    return pl.pallas_call(
        kernel,
        out_shape=jax.ShapeDtypeStruct((16, 32, 128), F32),
        in_specs=[pl.BlockSpec(memory_space=pltpu.HBM)] * 2,
        out_specs=pl.BlockSpec(memory_space=pltpu.VMEM),
        scratch_shapes=scratch,
        compiler_params=pltpu.CompilerParams(
            collective_id=0, has_side_effects=True, vmem_limit_bytes=24 * 2**20
        ),
        cost_estimate=pl.CostEstimate(flops=10_000_000, bytes_accessed=3 * 262144, transcendentals=0),
    )(pltpu.with_memory_space_constraint(right_side, pltpu.HBM), pltpu.with_memory_space_constraint(coefficient, pltpu.HBM))


def solution(mesh):
    return jax.shard_map(
        per_device,
        mesh=mesh,
        in_specs=(P("gx", "yz", None), P("gx", "yz", None)),
        out_specs=P("gx", "yz", None),
        check_vma=False,
    )
```

```python
import copy as copies

import jax
import jax.numpy as jnp
from jax import lax
from jax.experimental import pallas as pl
from jax.experimental.pallas import tpu as pltpu
from jax.sharding import PartitionSpec as P

MESH = pl.DeviceIdType.MESH
BITERS = 4
OMEGA = 0.8
NG = 8
NQ = 64
F32 = jnp.float32


def roll(v, by):
    return pltpu.roll(v, by % 128, 1)


def lanes_of(rows):
    return lax.broadcasted_iota(jnp.int32, (rows, 128), 1)


def pick(v, index):
    return jnp.take_along_axis(v, index, axis=1)


def swap(v, bit):
    lane = lanes_of(v.shape[0])
    return jnp.where((lane & bit) == 0, roll(v, -bit), roll(v, bit))


class Level:
    def __init__(self, scale, rows, start, unit, planes, depth, extent):
        self.half = 0.5 * scale
        self.rows = rows
        self.start = start
        self.unit = unit
        self.planes = planes
        self.depth = depth
        self.extent = extent

    def window(self, start, rows):
        other = copies.copy(self)
        other.start, other.rows = start, rows
        return other

    def load(self, ref, i, shift=0):
        return ref[i, pl.ds(self.start + shift, self.rows), :]

    def store(self, ref, i, v):
        ref[i, pl.ds(self.start, self.rows), :] = v

    def shifted(self, ref, i):
        c = self.load(ref, i)
        if self.planes == 1:
            xp, xm = self.load(ref, i + 1), self.load(ref, i - 1)
        else:
            s = self.unit
            bits = (self.planes - 1) * s
            field = lanes_of(self.rows) & bits
            xp = roll(jnp.where(field != 0, c, self.load(ref, i + 1)), -s)
            xm = roll(jnp.where(field != bits, c, self.load(ref, i - 1)), s)
        yp, ym = self.load(ref, i, 1), self.load(ref, i, -1)
        zp, zm = roll(c, -self.depth), roll(c, self.depth)
        return c, (xp, xm, yp, ym, zp, zm)

    def weigh(self, i):
        along = lanes_of(self.rows) & self.extent
        first, last = along == 0, along == self.extent
        c, others = self.shifted(self.b, i)
        total = None
        for k, other in enumerate(others):
            edge = {4: last, 5: first}.get(k)
            if edge is not None:
                other = jnp.where(edge, 0.0, other)
            w = self.half * (c + other)
            total = w if total is None else total + w
            if edge is not None:
                w = jnp.where(edge, 0.0, w)
            self.w[k, i, pl.ds(self.start, self.rows), :] = w
        self.store(self.d, i, total)
        inside = c > 0.0
        self.store(self.inv, i, jnp.where(inside, OMEGA / jnp.where(inside, total, 1.0), 0.0))

    def first(self, i):
        self.store(self.v, i, self.load(self.inv, i) * self.load(self.f, i))

    def around(self, ref, i):
        c, others = self.shifted(ref, i)
        total = None
        for k, other in enumerate(others):
            term = self.w[k, i, pl.ds(self.start, self.rows), :] * other
            total = term if total is None else total + term
        return c, total

    def smooth(self, src, i):
        c, s = self.around(src, i)
        return (1.0 - OMEGA) * c + self.load(self.inv, i) * (self.load(self.f, i) + s)

    def residual(self, i):
        c, s = self.around(self.u, i)
        return self.load(self.f, i) + s - self.load(self.d, i) * c


def each(lo, hi, body, group=None):
    if group is None:
        for i in range(lo, hi):
            body(i)
    else:
        assert (hi - lo) % group == 0

        def step(t, carry):
            for k in range(group):
                body(lo + t * group + k)
            return carry

        lax.fori_loop(0, (hi - lo) // group, step, 0)


R0, O0 = 56, 12
R1, O1 = 40, 12
R2, O2 = 40, 16
R3, O3 = 32, 16

LEVEL_SHAPES = ((22, R0), (10, R1), (10, R2), (10, R3))

GROUP_ROWS = ((6, 54), (13, 16), (16, 8), (16, 8), (5, 40), (4, 46), (3, 5), (3, 21), (3, 16))


def kernel(f_hbm, b_hbm, out, *refs):
    refs = list(refs)

    def take(n):
        got = refs[:n]
        del refs[:n]
        return got

    lv = [
        Level(1.0, 40, 8, 0, 1, 1, 127),
        Level(0.25, 24, 8, 64, 2, 1, 63),
        Level(0.0625, 24, 8, 32, 4, 1, 31),
        Level(0.015625, 16, 8, 64, 2, 2, 30),
    ]
    for one in lv:
        one.b, one.f, one.v, one.u, one.d, one.inv, one.w = take(7)
    pair, b2_own, f2_own, all_b4, all_f4, e_pad = take(6)
    load_sem, send_sem, recv_sem, ready = take(4)
    l0, l1, l2, l3 = lv

    g, q = lax.axis_index("gx"), lax.axis_index("yz")

    load_b = pltpu.make_async_copy(b_hbm, l0.b.at[pl.ds(3, 16), pl.ds(O0, 32)], load_sem.at[0])
    load_f = pltpu.make_async_copy(f_hbm, l0.f.at[pl.ds(3, 16), pl.ds(O0, 32)], load_sem.at[1])
    load_b.start()
    load_f.start()

    def device(dg, dq):
        return {"gx": g + dg & NG - 1, "yz": q + dq & NQ - 1}

    near = [(dg, dq) for dg in (-1, 1) for dq in (-1, 1)] + [(0, -1), (0, 1), (-1, 0), (1, 0)]
    wide = [(dg, dq) for dg in (4, 3, 5, 2, 6, 1, 7, 0) for dq in (-1, 1, 0) if dg or dq]

    def yz_order():
        order = []
        for d in range(1, NQ):
            z, x = d % 16, d // 16
            order.append((-(min(z, 16 - z) + min(x, 4 - x)), d))
        return [d for _, d in sorted(order)]

    far = yz_order()

    barrier = pltpu.get_barrier_semaphore()

    def greet(target):
        pl.semaphore_signal(barrier, inc=1, device_id=target, device_id_type=MESH)

    def device_xz(dx, dz):
        return {"gx": g, "yz": ((q >> 4) + dx & 3) * 16 + (q + dz & 15)}

    greeted = [device(dg, dq) for dg, dq in near]
    greeted += [device(dg, dq) for dg in (-2, 2) for dq in (-1, 0, 1)]
    greeted += [device_xz(0, dz) for dz in (1, -1, 2, -2, 3, -3)]
    greeted += [device_xz(dx, 0) for dx in (1, 2, 3)]
    for target in greeted:
        greet(target)

    for one, (blocks, rows) in ((l1, LEVEL_SHAPES[1]), (l2, LEVEL_SHAPES[2]), (l3, LEVEL_SHAPES[3])):
        for ref in (one.b, one.v, one.u):
            for i in (0, blocks - 1):
                ref[i] = jnp.zeros((rows, 128), F32)
    for ref in (l3.b, l3.f):
        for i in range(1, 9):
            ref[i] = jnp.zeros((R3, 128), F32)
    e_pad[pl.ds(0, 8), :] = jnp.zeros((8, 128), F32)
    e_pad[pl.ds(72, 8), :] = jnp.zeros((8, 128), F32)

    low = lanes_of(16) < 64
    pairs = 2 * (lanes_of(16) & 63)

    def restrict_0(make, store):
        def body(i):
            halves = []
            for half in range(2):
                slot = 2 * i + half
                pair[slot, pl.ds(0, 32), :] = make(2 * slot) + make(2 * slot + 1)
                t = pair[slot, pl.ds(0, 16, stride=2), :] + pair[slot, pl.ds(1, 16, stride=2), :]
                halves.append(pick(t, pairs) + pick(t, pairs + 1))
            store(i, 0.125 * jnp.where(low, halves[0], halves[1]))

        return body

    def restrict_1(make, rows):
        lane = lanes_of(rows)
        parts = []
        for i in range(4):
            pair[i, pl.ds(0, 2 * rows), :] = make(i)
            t = pair[i, pl.ds(0, rows, stride=2), :] + pair[i, pl.ds(1, rows, stride=2), :]
            parts.append(t + roll(t, 64))
        index = 2 * (lane & 31) + ((lane & 32) * 2)
        halves = []
        for i in (0, 2):
            t = jnp.where(lane < 64, parts[i], parts[i + 1])
            halves.append(pick(t, index) + pick(t, index + 1))
        return 0.125 * jnp.where(lane < 64, halves[0], halves[1])

    def restrict_2(make):
        def one(i):
            pair[i, pl.ds(0, 24), :] = make(i)
            t = pair[i, pl.ds(0, 12, stride=2), :] + pair[i, pl.ds(1, 12, stride=2), :]
            t = t + swap(t, 32)
            return 0.125 * (t + swap(t, 1))

        return one

    def restrict_3(make):
        k = lanes_of(1) & 15
        row = None
        for i in range(8):
            pair[i, pl.ds(0, 4), :] = make(i)
            t = pair[i, pl.ds(0, 2, stride=2), :] + pair[i, pl.ds(1, 2, stride=2), :]
            t = t + roll(t, 64)
            t = 0.125 * pick(t + swap(t, 2), (lanes_of(2) >> 4) * 4)
            for j in range(2):
                row = t[j : j + 1] if row is None else jnp.where(k == 2 * i + j, t[j : j + 1], row)
        return row

    load_b.wait()

    def store_b1(i, v):
        l1.b[3 + i, pl.ds(O1, 16), :] = v

    each(0, 4, restrict_0(lambda p: l0.b[3 + p, pl.ds(O0, 32), :], store_b1), 2)
    load_f.wait()

    core = l0.window(14, 28)
    each(4, 18, core.weigh, 7)
    each(4, 18, core.first, 7)
    core = l0.window(16, 24)
    each(5, 17, lambda i: core.store(l0.u, i, core.smooth(l0.v, i)), 6)
    rims = (l0.window(8, 8), l0.window(40, 8))

    def outside(lo, width, hi, work):
        def rim(i):
            for one in rims:
                work(one, i)

        each(lo + width, hi - width, rim, (hi - lo - 2 * width) // 2)
        for i in list(range(lo, lo + width)) + list(range(hi - width, hi)):
            work(l0, i)

    pl.semaphore_wait(barrier, len(greeted))

    def pass_on(n, targets):
        for target in targets:
            pl.semaphore_signal(ready.at[n], inc=1, device_id=target, device_id_type=MESH)


    def cut(d, first, size, width):
        if d == 0:
            return first, first, size
        if d > 0:
            return first + size - width, first - width, width
        return first, first + size, width

    def send_near(slot, ref, blocks, rows, block_width, row_width):
        for dg, dq in near:
            bs, bt, bn = cut(dg, blocks[0], blocks[1], block_width)
            rs, rt, rn = cut(dq, rows[0], rows[1], row_width)
            copy = pltpu.make_async_remote_copy(
                src_ref=ref.at[pl.ds(bs, bn), pl.ds(rs, rn)],
                dst_ref=ref.at[pl.ds(bt, bn), pl.ds(rt, rn)],
                send_sem=send_sem.at[slot],
                recv_sem=recv_sem.at[slot],
                device_id=device(dg, dq),
                device_id_type=MESH,
            )
            copy.start()

    def all_of(sem, shape):
        some = l0.w.at[(0,) + tuple(pl.ds(0, n) for n in shape)]
        return pltpu.make_async_copy(some, some, sem)

    def arrive(group):
        all_of(recv_sem.at[group], GROUP_ROWS[group]).wait()

    send_near(0, l0.b, (3, 16), (O0, 32), 3, 3)
    send_near(1, l0.f, (3, 16), (O0, 32), 2, 2)
    send_near(2, l1.b, (3, 4), (O1, 16), 2, 4)
    pass_on(
        0,
        [device(dg, dq) for dg in (-2, 2) for dq in (-1, 0, 1)]
        + [device_xz(0, dz) for dz in (3, -3)],
    )

    def clear(ref, blocks, rows, total_blocks, block_width, row_width):
        first, count = blocks
        start, height = rows

        @pl.when(g == 0)
        def _():
            for i in range(first - block_width, first):
                ref[i] = jnp.zeros(ref.shape[1:], F32)

        @pl.when(g == NG - 1)
        def _():
            for i in range(first + count, first + count + block_width):
                ref[i] = jnp.zeros(ref.shape[1:], F32)

        @pl.when(q == 0)
        def _():
            for i in range(first - block_width, first + count + block_width):
                ref[i, pl.ds(start - row_width, row_width), :] = jnp.zeros((row_width, 128), F32)

        @pl.when(q == NQ - 1)
        def _():
            for i in range(first - block_width, first + count + block_width):
                ref[i, pl.ds(start + height, row_width), :] = jnp.zeros((row_width, 128), F32)

    arrive(0)
    clear(l0.b, (3, 16), (O0, 32), 22, 3, 3)
    outside(1, 3, 21, lambda one, i: one.weigh(i))
    arrive(1)
    outside(1, 3, 21, lambda one, i: one.first(i))
    outside(2, 3, 20, lambda one, i: one.store(l0.u, i, one.smooth(l0.v, i)))

    def store_f1(i, v):
        l1.f[3 + i, pl.ds(O1, 16), :] = v

    each(0, 4, restrict_0(lambda p: l0.residual(3 + p)[O0 - 8 : O0 - 8 + 32], store_f1), 2)
    send_near(3, l1.f, (3, 4), (O1, 16), 2, 4)

    arrive(2)
    clear(l1.b, (3, 4), (O1, 16), 10, 2, 4)
    b2_own[pl.ds(7, 10), :] = restrict_1(lambda i: l1.b[3 + i, pl.ds(O1 - 2, 20), :], 10)

    def send_wide(slot, parts):
        for dg, dq in wide:
            src, dst = parts(dq)
            copy = pltpu.make_async_remote_copy(
                src_ref=src,
                dst_ref=dst,
                send_sem=send_sem.at[slot],
                recv_sem=recv_sem.at[slot],
                device_id=device(dg, dq),
                device_id_type=MESH,
            )
            copy.start()

    pl.semaphore_wait(ready.at[0], 8)

    def b2_parts(dq):
        src, dst, n = {0: (8, O2, 8), 1: (7, O2 - 9, 9), -1: (8, O2 + 8, 9)}[dq]
        return b2_own.at[pl.ds(src, n)], l2.b.at[1 + g, pl.ds(dst, n)]

    send_wide(4, b2_parts)
    pass_on(1, [device_xz(dx, dz) for dx in range(4) for dz in (3, -3)])
    l2.b[1 + g, pl.ds(O2, 8), :] = b2_own[pl.ds(8, 8), :]
    each(1, 9, l1.weigh, 4)
    arrive(3)
    each(1, 9, l1.first)
    each(2, 8, lambda i: l1.store(l1.u, i, l1.smooth(l1.v, i)))
    f2_own[...] = restrict_1(lambda i: l1.residual(3 + i)[O1 - 8 : O1 - 8 + 16], 8)

    def f2_parts(dq):
        return f2_own, l2.f.at[1 + g, pl.ds(O2 - 8 * dq, 8)]

    send_wide(5, f2_parts)
    l2.f[1 + g, pl.ds(O2, 8), :] = f2_own[...]

    arrive(4)

    @pl.when(q == 0)
    def _():
        for i in range(1, 9):
            l2.b[i, pl.ds(O2 - 9, 9), :] = jnp.zeros((9, 128), F32)

    @pl.when(q == NQ - 1)
    def _():
        for i in range(1, 9):
            l2.b[i, pl.ds(O2 + 8, 9), :] = jnp.zeros((9, 128), F32)

    each(1, 9, l2.weigh, 4)
    b3_of = restrict_2(lambda i: l2.load(l2.b, i))

    def store_b3(i):
        l3.b[i, pl.ds(O3 - 4, 12), :] = b3_of(i)

    each(1, 9, store_b3)
    each(1, 9, l3.weigh, 4)

    def send_rows(slot, ref, start, count, targets):
        here = ref.at[pl.ds(start, count)]
        for target in targets:
            copy = pltpu.make_async_remote_copy(
                src_ref=here,
                dst_ref=here,
                send_sem=send_sem.at[slot],
                recv_sem=recv_sem.at[slot],
                device_id=target,
                device_id_type=MESH,
            )
            copy.start()

    b4 = restrict_3(lambda i: l3.b[1 + i, pl.ds(O3, 4), :])
    pl.semaphore_wait(ready.at[1], 8)
    all_b4[pl.ds(q, 1), :] = b4
    send_rows(6, all_b4, q, 1, [device_xz(0, dz) for dz in (8, 7, 9, 6, 10, 5, 11, 4, 12, 3, 13, 2, 14, 1, 15)])

    arrive(5)
    each(1, 9, l2.first)
    each(1, 9, lambda i: l2.store(l2.u, i, l2.smooth(l2.v, i)))
    f3_of = restrict_2(l2.residual)

    def store_f3(i):
        l3.f[i, pl.ds(O3 - 4, 12), :] = f3_of(i)

    each(1, 9, store_f3)
    each(1, 9, l3.first)
    each(1, 9, lambda i: l3.store(l3.u, i, l3.smooth(l3.v, i)))
    f4 = restrict_3(lambda i: l3.residual(1 + i)[O3 - 8 : O3 - 8 + 4])

    all_f4[pl.ds(q, 1), :] = f4
    send_rows(7, all_f4, q, 1, [device(0, d) for d in far])
    arrive(6)
    send_rows(8, all_b4, pl.multiple_of((q >> 4) * 16, 16), 16, [device_xz(dx, 0) for dx in (2, 1, 3)])
    arrive(8)
    weight = all_b4[...]
    lane = lanes_of(NQ)
    row = lax.broadcasted_iota(jnp.int32, (NQ, 128), 0)
    odd = (lane & 1) == 1
    edges = (
        (lane & 14) == 14,
        (lane & 14) == 0,
        (row == NQ - 1) & odd,
        (row == 0) & jnp.logical_not(odd),
        lane >= 112,
        lane < 16,
    )

    def bottom_shifts(v):
        up, down = roll(v, -1), roll(v, 1)
        yp = jnp.where(odd, pltpu.roll(down, NQ - 1, 0), up)
        ym = jnp.where(odd, down, pltpu.roll(up, 1, 0))
        return roll(v, -2), roll(v, 2), yp, ym, roll(v, -16), roll(v, 16)

    half = 0.5 * 0.25**4
    bottom_w = []
    bottom_d = None
    for edge, other in zip(edges, bottom_shifts(weight)):
        w = half * (weight + jnp.where(edge, 0.0, other))
        bottom_d = w if bottom_d is None else bottom_d + w
        bottom_w.append(jnp.where(edge, 0.0, w))

    arrive(7)
    source = all_f4[...]

    def apply_op(v):
        result = bottom_d * v
        for w, other in zip(bottom_w, bottom_shifts(v)):
            result = result - w * other
        return result

    def total(v):
        return jnp.sum(v, keepdims=True)

    answer = None
    residual = source
    direction = source
    applied = None
    rho = total(source * source)
    alpha = omega = shadow_bent = None
    for turn in range(BITERS):
        if turn > 0:
            beta = -(alpha * shadow_bent) / rho
            rho = -(omega * shadow_bent)
            direction = residual + beta * (direction - omega * applied)
        applied = apply_op(direction)
        alpha = rho / total(source * applied)
        middle = residual - alpha * applied
        bent = apply_op(middle)
        omega = total(bent * middle) / total(bent * bent)
        shadow_bent = total(source * bent)
        step = alpha * direction + omega * middle
        answer = step if answer is None else answer + step
        residual = middle - omega * bent

    e_pad[pl.ds(8, NQ), :] = answer
    fine = lax.broadcasted_iota(jnp.int32, (16, 128), 0) - 8
    near_rows = jnp.where(
        fine < 0,
        e_pad[pl.ds(7 + q, 1), :],
        jnp.where(fine < 4, e_pad[pl.ds(8 + q, 1), :], e_pad[pl.ds(9 + q, 1), :]),
    )
    parity = jnp.where((fine < 0) | ((fine >= 2) & (fine < 4)), 1, 0)
    group = ((lanes_of(16) >> 2) & 7) * 16

    def up_3(i):
        wide_e = pick(near_rows, group + parity + 2 * (i - 1))
        l3.store(l3.v, i, l3.load(l3.u, i) + wide_e)

    each(1, 9, up_3)

    def up_3s(i):
        v = l3.smooth(l3.v, i)
        v = v[6:14]
        for k in range(2):
            pair[i, pl.ds(k, 8, stride=2), :] = v
        mid = l2.u[i, pl.ds(O2 - 4, 16), :] + pair[i, pl.ds(0, 16), :]
        l2.v[i, pl.ds(O2 - 4, 16), :] = mid

    each(1, 9, up_3s)
    each(1, 9, lambda i: l2.store(l2.u, i, l2.smooth(l2.v, i)))

    spread = (lanes_of(12) & 63) >> 1
    for i in range(-1, 5):
        from_block = 1 + g + (i // 4)
        v = pick(l2.u[from_block, pl.ds(O2 - 2, 12), :], spread + 32 * (i % 4))
        for k in range(2):
            pair[i + 1, pl.ds(k, 12, stride=2), :] = v
        l1.v[3 + i, pl.ds(O1 - 4, 24), :] = l1.u[3 + i, pl.ds(O1 - 4, 24), :] + pair[i + 1, pl.ds(0, 24), :]
    for i in range(-1, 5):
        l1.store(l1.u, 3 + i, l1.smooth(l1.v, 3 + i))

    spread = lanes_of(20) >> 1
    for i in range(-1, 9):
        v = l1.u[3 + (i // 2), pl.ds(O1 - 2, 20), :]
        v = pick(v, spread + 64 * (i % 2))
        for k in range(2):
            pair[i + 1, pl.ds(k, 20, stride=2), :] = v
        wide_v = pair[i + 1, pl.ds(0, 40), :]
        for p in (2 * i, 2 * i + 1):
            if -1 <= p <= 16:
                l0.store(l0.v, 3 + p, l0.load(l0.u, 3 + p) + wide_v)

    def finish(p):
        out[p] = l0.smooth(l0.v, 3 + p)[O0 - 8 : O0 - 8 + 32]

    each(0, 16, finish, 8)

    for group, shape in enumerate(GROUP_ROWS):
        all_of(send_sem.at[group], shape).wait()


def per_device(right_side, coefficient):
    scratch = []
    for blocks, rows in LEVEL_SHAPES:
        scratch += [pltpu.VMEM((blocks, rows, 128), F32)] * 6
        scratch.append(pltpu.VMEM((6, blocks, rows, 128), F32))
    scratch += [
        pltpu.VMEM((16, 48, 128), F32),
        pltpu.VMEM((24, 128), F32),
        pltpu.VMEM((8, 128), F32),
        pltpu.VMEM((NQ, 128), F32),
        pltpu.VMEM((NQ, 128), F32),
        pltpu.VMEM((80, 128), F32),
        pltpu.SemaphoreType.DMA((2,)),
        pltpu.SemaphoreType.DMA((9,)),
        pltpu.SemaphoreType.DMA((9,)),
        pltpu.SemaphoreType.REGULAR((2,)),
    ]
    return pl.pallas_call(
        kernel,
        out_shape=jax.ShapeDtypeStruct((16, 32, 128), F32),
        in_specs=[pl.BlockSpec(memory_space=pltpu.HBM)] * 2,
        out_specs=pl.BlockSpec(memory_space=pltpu.VMEM),
        scratch_shapes=scratch,
        compiler_params=pltpu.CompilerParams(
            collective_id=0, has_side_effects=True, vmem_limit_bytes=24 * 2**20
        ),
        cost_estimate=pl.CostEstimate(flops=10_000_000, bytes_accessed=3 * 262144, transcendentals=0),
    )(pltpu.with_memory_space_constraint(right_side, pltpu.HBM), pltpu.with_memory_space_constraint(coefficient, pltpu.HBM))


def solution(mesh):
    return jax.shard_map(
        per_device,
        mesh=mesh,
        in_specs=(P("gx", "yz", None), P("gx", "yz", None)),
        out_specs=P("gx", "yz", None),
        check_vma=False,
    )
```

```python
import copy as copies

import jax
import jax.numpy as jnp
from jax import lax
from jax.experimental import pallas as pl
from jax.experimental.pallas import tpu as pltpu
from jax.sharding import PartitionSpec as P

MESH = pl.DeviceIdType.MESH
BITERS = 4
OMEGA = 0.8
NG = 8
NQ = 64
F32 = jnp.float32


def roll(v, by):
    return pltpu.roll(v, by % 128, 1)


def lanes_of(rows):
    return lax.broadcasted_iota(jnp.int32, (rows, 128), 1)


def pick(v, index):
    return jnp.take_along_axis(v, index, axis=1)


def swap(v, bit):
    lane = lanes_of(v.shape[0])
    return jnp.where((lane & bit) == 0, roll(v, -bit), roll(v, bit))


class Level:
    def __init__(self, scale, rows, start, unit, planes, depth, extent):
        self.half = 0.5 * scale
        self.rows = rows
        self.start = start
        self.unit = unit
        self.planes = planes
        self.depth = depth
        self.extent = extent

    def window(self, start, rows):
        other = copies.copy(self)
        other.start, other.rows = start, rows
        return other

    def load(self, ref, i, shift=0):
        return ref[i, pl.ds(self.start + shift, self.rows), :]

    def store(self, ref, i, v):
        ref[i, pl.ds(self.start, self.rows), :] = v

    def shifted(self, ref, i):
        c = self.load(ref, i)
        if self.planes == 1:
            xp, xm = self.load(ref, i + 1), self.load(ref, i - 1)
        else:
            s = self.unit
            bits = (self.planes - 1) * s
            field = lanes_of(self.rows) & bits
            xp = roll(jnp.where(field != 0, c, self.load(ref, i + 1)), -s)
            xm = roll(jnp.where(field != bits, c, self.load(ref, i - 1)), s)
        yp, ym = self.load(ref, i, 1), self.load(ref, i, -1)
        zp, zm = roll(c, -self.depth), roll(c, self.depth)
        return c, (xp, xm, yp, ym, zp, zm)

    def weigh(self, i):
        along = lanes_of(self.rows) & self.extent
        first, last = along == 0, along == self.extent
        c, others = self.shifted(self.b, i)
        total = None
        for k, other in enumerate(others):
            edge = {4: last, 5: first}.get(k)
            if edge is not None:
                other = jnp.where(edge, 0.0, other)
            w = self.half * (c + other)
            total = w if total is None else total + w
            if edge is not None:
                w = jnp.where(edge, 0.0, w)
            self.w[k, i, pl.ds(self.start, self.rows), :] = w
        self.store(self.d, i, total)
        inside = c > 0.0
        self.store(self.inv, i, jnp.where(inside, OMEGA / jnp.where(inside, total, 1.0), 0.0))

    def first(self, i):
        self.store(self.v, i, self.load(self.inv, i) * self.load(self.f, i))

    def around(self, ref, i):
        c, others = self.shifted(ref, i)
        total = None
        for k, other in enumerate(others):
            term = self.w[k, i, pl.ds(self.start, self.rows), :] * other
            total = term if total is None else total + term
        return c, total

    def smooth(self, src, i):
        c, s = self.around(src, i)
        return (1.0 - OMEGA) * c + self.load(self.inv, i) * (self.load(self.f, i) + s)

    def residual(self, i):
        c, s = self.around(self.u, i)
        return self.load(self.f, i) + s - self.load(self.d, i) * c


def each(lo, hi, body, group=None):
    if group is None:
        for i in range(lo, hi):
            body(i)
    else:
        assert (hi - lo) % group == 0

        def step(t, carry):
            for k in range(group):
                body(lo + t * group + k)
            return carry

        lax.fori_loop(0, (hi - lo) // group, step, 0)


R0, O0 = 56, 12
R1, O1 = 40, 12
R2, O2 = 40, 16
R3, O3 = 32, 16

LEVEL_SHAPES = ((22, R0), (10, R1), (10, R2), (10, R3))

GROUP_ROWS = ((6, 54), (13, 16), (16, 8), (16, 8), (5, 40), (4, 46), (3, 5), (3, 21), (3, 16))


def kernel(f_hbm, b_hbm, out, *refs):
    refs = list(refs)

    def take(n):
        got = refs[:n]
        del refs[:n]
        return got

    lv = [
        Level(1.0, 40, 8, 0, 1, 1, 127),
        Level(0.25, 24, 8, 64, 2, 1, 63),
        Level(0.0625, 24, 8, 32, 4, 1, 31),
        Level(0.015625, 16, 8, 64, 2, 2, 30),
    ]
    for one in lv:
        one.b, one.f, one.v, one.u, one.d, one.inv, one.w = take(7)
    pair, b2_own, f2_own, all_b4, all_f4, e_pad = take(6)
    load_sem, send_sem, recv_sem, ready = take(4)
    l0, l1, l2, l3 = lv

    g, q = lax.axis_index("gx"), lax.axis_index("yz")

    load_b = pltpu.make_async_copy(b_hbm, l0.b.at[pl.ds(3, 16), pl.ds(O0, 32)], load_sem.at[0])
    load_f = pltpu.make_async_copy(f_hbm, l0.f.at[pl.ds(3, 16), pl.ds(O0, 32)], load_sem.at[1])
    load_b.start()
    load_f.start()

    def device(dg, dq):
        return {"gx": g + dg & NG - 1, "yz": q + dq & NQ - 1}

    near = [(dg, dq) for dg in (-1, 1) for dq in (-1, 1)] + [(0, -1), (0, 1), (-1, 0), (1, 0)]
    wide = [(dg, dq) for dg in (4, 3, 5, 2, 6, 1, 7, 0) for dq in (-1, 1, 0) if dg or dq]

    def yz_order():
        order = []
        for d in range(1, NQ):
            z, x = d % 16, d // 16
            order.append((-(min(z, 16 - z) + min(x, 4 - x)), d))
        return [d for _, d in sorted(order)]

    far = yz_order()

    barrier = pltpu.get_barrier_semaphore()

    def greet(target):
        pl.semaphore_signal(barrier, inc=1, device_id=target, device_id_type=MESH)

    def device_xz(dx, dz):
        return {"gx": g, "yz": ((q >> 4) + dx & 3) * 16 + (q + dz & 15)}

    greeted = [device(dg, dq) for dg, dq in near]
    greeted += [device(dg, dq) for dg in (-2, 2) for dq in (-1, 0, 1)]
    greeted += [device_xz(0, dz) for dz in (1, -1, 2, -2, 3, -3)]
    greeted += [device_xz(dx, 0) for dx in (1, 2, 3)]
    for target in greeted:
        greet(target)

    for one, (blocks, rows) in ((l1, LEVEL_SHAPES[1]), (l2, LEVEL_SHAPES[2]), (l3, LEVEL_SHAPES[3])):
        for ref in (one.b, one.v, one.u):
            for i in (0, blocks - 1):
                ref[i] = jnp.zeros((rows, 128), F32)
    for ref in (l3.b, l3.f):
        for i in range(1, 9):
            ref[i] = jnp.zeros((R3, 128), F32)
    e_pad[pl.ds(0, 8), :] = jnp.zeros((8, 128), F32)
    e_pad[pl.ds(72, 8), :] = jnp.zeros((8, 128), F32)

    low = lanes_of(16) < 64
    pairs = 2 * (lanes_of(16) & 63)

    def restrict_0(make, store):
        def body(i):
            halves = []
            for half in range(2):
                slot = 2 * i + half
                pair[slot, pl.ds(0, 32), :] = make(2 * slot) + make(2 * slot + 1)
                t = pair[slot, pl.ds(0, 16, stride=2), :] + pair[slot, pl.ds(1, 16, stride=2), :]
                halves.append(pick(t, pairs) + pick(t, pairs + 1))
            store(i, 0.125 * jnp.where(low, halves[0], halves[1]))

        return body

    def restrict_1(make, rows):
        lane = lanes_of(rows)
        parts = []
        for i in range(4):
            pair[i, pl.ds(0, 2 * rows), :] = make(i)
            t = pair[i, pl.ds(0, rows, stride=2), :] + pair[i, pl.ds(1, rows, stride=2), :]
            parts.append(t + roll(t, 64))
        index = 2 * (lane & 31) + ((lane & 32) * 2)
        halves = []
        for i in (0, 2):
            t = jnp.where(lane < 64, parts[i], parts[i + 1])
            halves.append(pick(t, index) + pick(t, index + 1))
        return 0.125 * jnp.where(lane < 64, halves[0], halves[1])

    def restrict_2(make):
        def one(i):
            pair[i, pl.ds(0, 24), :] = make(i)
            t = pair[i, pl.ds(0, 12, stride=2), :] + pair[i, pl.ds(1, 12, stride=2), :]
            t = t + swap(t, 32)
            return 0.125 * (t + swap(t, 1))

        return one

    def restrict_3(make):
        k = lanes_of(1) & 15
        row = None
        for i in range(8):
            pair[i, pl.ds(0, 4), :] = make(i)
            t = pair[i, pl.ds(0, 2, stride=2), :] + pair[i, pl.ds(1, 2, stride=2), :]
            t = t + roll(t, 64)
            t = 0.125 * pick(t + swap(t, 2), (lanes_of(2) >> 4) * 4)
            for j in range(2):
                row = t[j : j + 1] if row is None else jnp.where(k == 2 * i + j, t[j : j + 1], row)
        return row

    load_b.wait()


    pl.semaphore_wait(barrier, len(greeted))

    def pass_on(n, targets):
        for target in targets:
            pl.semaphore_signal(ready.at[n], inc=1, device_id=target, device_id_type=MESH)


    def cut(d, first, size, width):
        if d == 0:
            return first, first, size
        if d > 0:
            return first + size - width, first - width, width
        return first, first + size, width

    def send_near(slot, ref, blocks, rows, block_width, row_width):
        for dg, dq in near:
            bs, bt, bn = cut(dg, blocks[0], blocks[1], block_width)
            rs, rt, rn = cut(dq, rows[0], rows[1], row_width)
            copy = pltpu.make_async_remote_copy(
                src_ref=ref.at[pl.ds(bs, bn), pl.ds(rs, rn)],
                dst_ref=ref.at[pl.ds(bt, bn), pl.ds(rt, rn)],
                send_sem=send_sem.at[slot],
                recv_sem=recv_sem.at[slot],
                device_id=device(dg, dq),
                device_id_type=MESH,
            )
            copy.start()

    def all_of(sem, shape):
        some = l0.w.at[(0,) + tuple(pl.ds(0, n) for n in shape)]
        return pltpu.make_async_copy(some, some, sem)

    def arrive(group):
        all_of(recv_sem.at[group], GROUP_ROWS[group]).wait()

    send_near(0, l0.b, (3, 16), (O0, 32), 3, 3)
    load_f.wait()
    send_near(1, l0.f, (3, 16), (O0, 32), 2, 2)
    pass_on(
        0,
        [device(dg, dq) for dg in (-2, 2) for dq in (-1, 0, 1)]
        + [device_xz(0, dz) for dz in (3, -3)],
    )

    def clear(ref, blocks, rows, total_blocks, block_width, row_width):
        first, count = blocks
        start, height = rows

        @pl.when(g == 0)
        def _():
            for i in range(first - block_width, first):
                ref[i] = jnp.zeros(ref.shape[1:], F32)

        @pl.when(g == NG - 1)
        def _():
            for i in range(first + count, first + count + block_width):
                ref[i] = jnp.zeros(ref.shape[1:], F32)

        @pl.when(q == 0)
        def _():
            for i in range(first - block_width, first + count + block_width):
                ref[i, pl.ds(start - row_width, row_width), :] = jnp.zeros((row_width, 128), F32)

        @pl.when(q == NQ - 1)
        def _():
            for i in range(first - block_width, first + count + block_width):
                ref[i, pl.ds(start + height, row_width), :] = jnp.zeros((row_width, 128), F32)

    def store_b1(i, v):
        l1.b[3 + i, pl.ds(O1, 16), :] = v

    each(0, 4, restrict_0(lambda p: l0.b[3 + p, pl.ds(O0, 32), :], store_b1), 2)
    send_near(2, l1.b, (3, 4), (O1, 16), 2, 4)

    core = l0.window(14, 28)
    each(4, 18, core.weigh, 7)
    each(4, 18, core.first, 7)
    core = l0.window(16, 24)
    each(5, 17, lambda i: core.store(l0.u, i, core.smooth(l0.v, i)), 6)
    rims = (l0.window(8, 8), l0.window(40, 8))

    def outside(lo, width, hi, work):
        def rim(i):
            for one in rims:
                work(one, i)

        each(lo + width, hi - width, rim, (hi - lo - 2 * width) // 2)
        for i in list(range(lo, lo + width)) + list(range(hi - width, hi)):
            work(l0, i)

    arrive(0)
    clear(l0.b, (3, 16), (O0, 32), 22, 3, 3)
    outside(1, 3, 21, lambda one, i: one.weigh(i))
    arrive(1)
    outside(1, 3, 21, lambda one, i: one.first(i))
    outside(2, 3, 20, lambda one, i: one.store(l0.u, i, one.smooth(l0.v, i)))

    def store_f1(i, v):
        l1.f[3 + i, pl.ds(O1, 16), :] = v

    each(0, 4, restrict_0(lambda p: l0.residual(3 + p)[O0 - 8 : O0 - 8 + 32], store_f1), 2)
    send_near(3, l1.f, (3, 4), (O1, 16), 2, 4)

    arrive(2)
    clear(l1.b, (3, 4), (O1, 16), 10, 2, 4)
    b2_own[pl.ds(7, 10), :] = restrict_1(lambda i: l1.b[3 + i, pl.ds(O1 - 2, 20), :], 10)

    def send_wide(slot, parts):
        for dg, dq in wide:
            src, dst = parts(dq)
            copy = pltpu.make_async_remote_copy(
                src_ref=src,
                dst_ref=dst,
                send_sem=send_sem.at[slot],
                recv_sem=recv_sem.at[slot],
                device_id=device(dg, dq),
                device_id_type=MESH,
            )
            copy.start()

    pl.semaphore_wait(ready.at[0], 8)

    def b2_parts(dq):
        src, dst, n = {0: (8, O2, 8), 1: (7, O2 - 9, 9), -1: (8, O2 + 8, 9)}[dq]
        return b2_own.at[pl.ds(src, n)], l2.b.at[1 + g, pl.ds(dst, n)]

    send_wide(4, b2_parts)
    pass_on(1, [device_xz(dx, dz) for dx in range(4) for dz in (3, -3)])
    l2.b[1 + g, pl.ds(O2, 8), :] = b2_own[pl.ds(8, 8), :]
    each(1, 9, l1.weigh)
    arrive(3)
    each(1, 9, l1.first)
    each(2, 8, lambda i: l1.store(l1.u, i, l1.smooth(l1.v, i)))
    f2_own[...] = restrict_1(lambda i: l1.residual(3 + i)[O1 - 8 : O1 - 8 + 16], 8)

    def f2_parts(dq):
        return f2_own, l2.f.at[1 + g, pl.ds(O2 - 8 * dq, 8)]

    send_wide(5, f2_parts)
    l2.f[1 + g, pl.ds(O2, 8), :] = f2_own[...]

    arrive(4)

    @pl.when(q == 0)
    def _():
        for i in range(1, 9):
            l2.b[i, pl.ds(O2 - 9, 9), :] = jnp.zeros((9, 128), F32)

    @pl.when(q == NQ - 1)
    def _():
        for i in range(1, 9):
            l2.b[i, pl.ds(O2 + 8, 9), :] = jnp.zeros((9, 128), F32)

    each(1, 9, l2.weigh)
    b3_of = restrict_2(lambda i: l2.load(l2.b, i))

    def store_b3(i):
        l3.b[i, pl.ds(O3 - 4, 12), :] = b3_of(i)

    each(1, 9, store_b3)
    each(1, 9, l3.weigh)

    def send_rows(slot, ref, start, count, targets):
        here = ref.at[pl.ds(start, count)]
        for target in targets:
            copy = pltpu.make_async_remote_copy(
                src_ref=here,
                dst_ref=here,
                send_sem=send_sem.at[slot],
                recv_sem=recv_sem.at[slot],
                device_id=target,
                device_id_type=MESH,
            )
            copy.start()

    b4 = restrict_3(lambda i: l3.b[1 + i, pl.ds(O3, 4), :])
    pl.semaphore_wait(ready.at[1], 8)
    all_b4[pl.ds(q, 1), :] = b4
    send_rows(6, all_b4, q, 1, [device_xz(0, dz) for dz in (8, 7, 9, 6, 10, 5, 11, 4, 12, 3, 13, 2, 14, 1, 15)])

    arrive(5)
    each(1, 9, l2.first)
    each(1, 9, lambda i: l2.store(l2.u, i, l2.smooth(l2.v, i)))
    f3_of = restrict_2(l2.residual)

    def store_f3(i):
        l3.f[i, pl.ds(O3 - 4, 12), :] = f3_of(i)

    each(1, 9, store_f3)
    each(1, 9, l3.first)
    each(1, 9, lambda i: l3.store(l3.u, i, l3.smooth(l3.v, i)))
    f4 = restrict_3(lambda i: l3.residual(1 + i)[O3 - 8 : O3 - 8 + 4])

    all_f4[pl.ds(q, 1), :] = f4
    send_rows(7, all_f4, q, 1, [device(0, d) for d in far])
    arrive(6)
    send_rows(8, all_b4, pl.multiple_of((q >> 4) * 16, 16), 16, [device_xz(dx, 0) for dx in (2, 1, 3)])
    arrive(8)
    weight = all_b4[...]
    lane = lanes_of(NQ)
    row = lax.broadcasted_iota(jnp.int32, (NQ, 128), 0)
    odd = (lane & 1) == 1
    edges = (
        (lane & 14) == 14,
        (lane & 14) == 0,
        (row == NQ - 1) & odd,
        (row == 0) & jnp.logical_not(odd),
        lane >= 112,
        lane < 16,
    )

    def bottom_shifts(v):
        up, down = roll(v, -1), roll(v, 1)
        yp = jnp.where(odd, pltpu.roll(down, NQ - 1, 0), up)
        ym = jnp.where(odd, down, pltpu.roll(up, 1, 0))
        return roll(v, -2), roll(v, 2), yp, ym, roll(v, -16), roll(v, 16)

    half = 0.5 * 0.25**4
    bottom_w = []
    bottom_d = None
    for edge, other in zip(edges, bottom_shifts(weight)):
        w = half * (weight + jnp.where(edge, 0.0, other))
        bottom_d = w if bottom_d is None else bottom_d + w
        bottom_w.append(jnp.where(edge, 0.0, w))

    arrive(7)
    source = all_f4[...]

    def apply_op(v):
        result = bottom_d * v
        for w, other in zip(bottom_w, bottom_shifts(v)):
            result = result - w * other
        return result

    def total(v):
        return jnp.sum(v, keepdims=True)

    answer = None
    residual = source
    direction = source
    applied = None
    rho = total(source * source)
    alpha = omega = shadow_bent = None
    for turn in range(BITERS):
        if turn > 0:
            beta = -(alpha * shadow_bent) / rho
            rho = -(omega * shadow_bent)
            direction = residual + beta * (direction - omega * applied)
        applied = apply_op(direction)
        alpha = rho / total(source * applied)
        middle = residual - alpha * applied
        bent = apply_op(middle)
        omega = total(bent * middle) / total(bent * bent)
        shadow_bent = total(source * bent)
        step = alpha * direction + omega * middle
        answer = step if answer is None else answer + step
        residual = middle - omega * bent

    e_pad[pl.ds(8, NQ), :] = answer
    fine = lax.broadcasted_iota(jnp.int32, (16, 128), 0) - 8
    near_rows = jnp.where(
        fine < 0,
        e_pad[pl.ds(7 + q, 1), :],
        jnp.where(fine < 4, e_pad[pl.ds(8 + q, 1), :], e_pad[pl.ds(9 + q, 1), :]),
    )
    parity = jnp.where((fine < 0) | ((fine >= 2) & (fine < 4)), 1, 0)
    group = ((lanes_of(16) >> 2) & 7) * 16

    def up_3(i):
        wide_e = pick(near_rows, group + parity + 2 * (i - 1))
        l3.store(l3.v, i, l3.load(l3.u, i) + wide_e)

    each(1, 9, up_3)

    def up_3s(i):
        v = l3.smooth(l3.v, i)
        v = v[6:14]
        for k in range(2):
            pair[i, pl.ds(k, 8, stride=2), :] = v
        mid = l2.u[i, pl.ds(O2 - 4, 16), :] + pair[i, pl.ds(0, 16), :]
        l2.v[i, pl.ds(O2 - 4, 16), :] = mid

    each(1, 9, up_3s)
    each(1, 9, lambda i: l2.store(l2.u, i, l2.smooth(l2.v, i)))

    spread = (lanes_of(12) & 63) >> 1
    for i in range(-1, 5):
        from_block = 1 + g + (i // 4)
        v = pick(l2.u[from_block, pl.ds(O2 - 2, 12), :], spread + 32 * (i % 4))
        for k in range(2):
            pair[i + 1, pl.ds(k, 12, stride=2), :] = v
        l1.v[3 + i, pl.ds(O1 - 4, 24), :] = l1.u[3 + i, pl.ds(O1 - 4, 24), :] + pair[i + 1, pl.ds(0, 24), :]
    for i in range(-1, 5):
        l1.store(l1.u, 3 + i, l1.smooth(l1.v, 3 + i))

    spread = lanes_of(20) >> 1
    for i in range(-1, 9):
        v = l1.u[3 + (i // 2), pl.ds(O1 - 2, 20), :]
        v = pick(v, spread + 64 * (i % 2))
        for k in range(2):
            pair[i + 1, pl.ds(k, 20, stride=2), :] = v
        wide_v = pair[i + 1, pl.ds(0, 40), :]
        for p in (2 * i, 2 * i + 1):
            if -1 <= p <= 16:
                l0.store(l0.v, 3 + p, l0.load(l0.u, 3 + p) + wide_v)

    def finish(p):
        out[p] = l0.smooth(l0.v, 3 + p)[O0 - 8 : O0 - 8 + 32]

    each(0, 16, finish, 8)

    for group, shape in enumerate(GROUP_ROWS):
        all_of(send_sem.at[group], shape).wait()


def per_device(right_side, coefficient):
    scratch = []
    for blocks, rows in LEVEL_SHAPES:
        scratch += [pltpu.VMEM((blocks, rows, 128), F32)] * 6
        scratch.append(pltpu.VMEM((6, blocks, rows, 128), F32))
    scratch += [
        pltpu.VMEM((16, 48, 128), F32),
        pltpu.VMEM((24, 128), F32),
        pltpu.VMEM((8, 128), F32),
        pltpu.VMEM((NQ, 128), F32),
        pltpu.VMEM((NQ, 128), F32),
        pltpu.VMEM((80, 128), F32),
        pltpu.SemaphoreType.DMA((2,)),
        pltpu.SemaphoreType.DMA((9,)),
        pltpu.SemaphoreType.DMA((9,)),
        pltpu.SemaphoreType.REGULAR((2,)),
    ]
    return pl.pallas_call(
        kernel,
        out_shape=jax.ShapeDtypeStruct((16, 32, 128), F32),
        in_specs=[pl.BlockSpec(memory_space=pltpu.HBM)] * 2,
        out_specs=pl.BlockSpec(memory_space=pltpu.VMEM),
        scratch_shapes=scratch,
        compiler_params=pltpu.CompilerParams(
            collective_id=0, has_side_effects=True, vmem_limit_bytes=24 * 2**20
        ),
        cost_estimate=pl.CostEstimate(flops=10_000_000, bytes_accessed=3 * 262144, transcendentals=0),
    )(pltpu.with_memory_space_constraint(right_side, pltpu.HBM), pltpu.with_memory_space_constraint(coefficient, pltpu.HBM))


def solution(mesh):
    return jax.shard_map(
        per_device,
        mesh=mesh,
        in_specs=(P("gx", "yz", None), P("gx", "yz", None)),
        out_specs=P("gx", "yz", None),
        check_vma=False,
    )
```

```python
import copy as copies

import jax
import jax.numpy as jnp
from jax import lax
from jax.experimental import pallas as pl
from jax.experimental.pallas import tpu as pltpu
from jax.sharding import PartitionSpec as P

MESH = pl.DeviceIdType.MESH
BITERS = 4
OMEGA = 0.8
NG = 8
NQ = 64
F32 = jnp.float32


def roll(v, by):
    return pltpu.roll(v, by % 128, 1)


def lanes_of(rows):
    return lax.broadcasted_iota(jnp.int32, (rows, 128), 1)


def pick(v, index):
    return jnp.take_along_axis(v, index, axis=1)


class Level:
    def __init__(self, scale, rows, start, unit, planes, depth, extent):
        self.half = 0.5 * scale
        self.rows = rows
        self.start = start
        self.unit = unit
        self.planes = planes
        self.depth = depth
        self.extent = extent

    def window(self, start, rows):
        other = copies.copy(self)
        other.start, other.rows = start, rows
        return other

    def load(self, ref, i, shift=0):
        return ref[i, pl.ds(self.start + shift, self.rows), :]

    def store(self, ref, i, v):
        ref[i, pl.ds(self.start, self.rows), :] = v

    def shifted(self, ref, i):
        c = self.load(ref, i)
        if self.planes == 1:
            xp, xm = self.load(ref, i + 1), self.load(ref, i - 1)
        else:
            s = self.unit
            bits = (self.planes - 1) * s
            field = lanes_of(self.rows) & bits
            xp = roll(jnp.where(field != 0, c, self.load(ref, i + 1)), -s)
            xm = roll(jnp.where(field != bits, c, self.load(ref, i - 1)), s)
        yp, ym = self.load(ref, i, 1), self.load(ref, i, -1)
        zp, zm = roll(c, -self.depth), roll(c, self.depth)
        return c, (xp, xm, yp, ym, zp, zm)

    def weigh(self, i):
        along = lanes_of(self.rows) & self.extent
        first, last = along == 0, along == self.extent
        c, others = self.shifted(self.b, i)
        total = None
        for k, other in enumerate(others):
            edge = {4: last, 5: first}.get(k)
            if edge is not None:
                other = jnp.where(edge, 0.0, other)
            w = self.half * (c + other)
            total = w if total is None else total + w
            if edge is not None:
                w = jnp.where(edge, 0.0, w)
            self.w[k, i, pl.ds(self.start, self.rows), :] = w
        self.store(self.d, i, total)
        inside = c > 0.0
        self.store(self.inv, i, jnp.where(inside, OMEGA / jnp.where(inside, total, 1.0), 0.0))

    def first(self, i):
        self.store(self.v, i, self.load(self.inv, i) * self.load(self.f, i))

    def around(self, ref, i):
        c, others = self.shifted(ref, i)
        total = None
        for k, other in enumerate(others):
            term = self.w[k, i, pl.ds(self.start, self.rows), :] * other
            total = term if total is None else total + term
        return c, total

    def smooth(self, src, i):
        c, s = self.around(src, i)
        return (1.0 - OMEGA) * c + self.load(self.inv, i) * (self.load(self.f, i) + s)

    def residual(self, i):
        c, s = self.around(self.u, i)
        return self.load(self.f, i) + s - self.load(self.d, i) * c


def each(lo, hi, body, group=None):
    if group is None:
        for i in range(lo, hi):
            body(i)
    else:
        assert (hi - lo) % group == 0

        def step(t, carry):
            for k in range(group):
                body(lo + t * group + k)
            return carry

        lax.fori_loop(0, (hi - lo) // group, step, 0)


R0, O0 = 56, 12
R1, O1 = 40, 12
R2, O2 = 40, 16
R3, O3 = 32, 16

LEVEL_SHAPES = ((22, R0), (10, R1), (10, R2), (10, R3))

GROUP_ROWS = ((6, 54), (13, 16), (16, 8), (16, 8), (5, 40), (4, 46), (3, 5), (3, 21), (3, 16))


def kernel(f_hbm, b_hbm, out, *refs):
    refs = list(refs)

    def take(n):
        got = refs[:n]
        del refs[:n]
        return got

    lv = [
        Level(1.0, 40, 8, 0, 1, 1, 127),
        Level(0.25, 24, 8, 64, 2, 1, 63),
        Level(0.0625, 24, 8, 32, 4, 1, 31),
        Level(0.015625, 16, 8, 64, 2, 2, 30),
    ]
    for one in lv:
        one.b, one.f, one.v, one.u, one.d, one.inv, one.w = take(7)
    pair, b2_own, f2_own, all_b4, all_f4, e_pad = take(6)
    load_sem, send_sem, recv_sem, ready = take(4)
    l0, l1, l2, l3 = lv

    g, q = lax.axis_index("gx"), lax.axis_index("yz")

    load_b = pltpu.make_async_copy(b_hbm, l0.b.at[pl.ds(3, 16), pl.ds(O0, 32)], load_sem.at[0])
    load_f = pltpu.make_async_copy(f_hbm, l0.f.at[pl.ds(3, 16), pl.ds(O0, 32)], load_sem.at[1])
    load_b.start()
    load_f.start()

    def device(dg, dq):
        return {"gx": g + dg & NG - 1, "yz": q + dq & NQ - 1}

    near = [(dg, dq) for dg in (-1, 1) for dq in (-1, 1)] + [(0, -1), (0, 1), (-1, 0), (1, 0)]
    wide = [(dg, dq) for dg in (4, 3, 5, 2, 6, 1, 7, 0) for dq in (-1, 1, 0) if dg or dq]

    def yz_order():
        order = []
        for d in range(1, NQ):
            z, x = d % 16, d // 16
            order.append((-(min(z, 16 - z) + min(x, 4 - x)), d))
        return [d for _, d in sorted(order)]

    far = yz_order()

    barrier = pltpu.get_barrier_semaphore()

    def greet(target):
        pl.semaphore_signal(barrier, inc=1, device_id=target, device_id_type=MESH)

    def device_xz(dx, dz):
        return {"gx": g, "yz": ((q >> 4) + dx & 3) * 16 + (q + dz & 15)}

    greeted = [device(dg, dq) for dg, dq in near]
    greeted += [device(dg, dq) for dg in (-2, 2) for dq in (-1, 0, 1)]
    greeted += [device_xz(0, dz) for dz in (1, -1, 2, -2, 3, -3)]
    greeted += [device_xz(dx, 0) for dx in (1, 2, 3)]
    for target in greeted:
        greet(target)

    for one, (blocks, rows) in ((l1, LEVEL_SHAPES[1]), (l2, LEVEL_SHAPES[2]), (l3, LEVEL_SHAPES[3])):
        for ref in (one.b, one.v, one.u):
            for i in (0, blocks - 1):
                ref[i] = jnp.zeros((rows, 128), F32)
    for ref in (l3.b, l3.f):
        for i in range(1, 9):
            ref[i] = jnp.zeros((R3, 128), F32)
    e_pad[pl.ds(0, 8), :] = jnp.zeros((8, 128), F32)
    e_pad[pl.ds(72, 8), :] = jnp.zeros((8, 128), F32)

    low = lanes_of(16) < 64
    pairs = 2 * (lanes_of(16) & 63)

    def restrict_0(make, store):
        def body(i):
            halves = []
            for half in range(2):
                slot = 2 * i + half
                pair[slot, pl.ds(0, 32), :] = make(2 * slot) + make(2 * slot + 1)
                t = pair[slot, pl.ds(0, 16, stride=2), :] + pair[slot, pl.ds(1, 16, stride=2), :]
                halves.append(pick(t, pairs) + pick(t, pairs + 1))
            store(i, 0.125 * jnp.where(low, halves[0], halves[1]))

        return body

    def restrict_1(make, rows):
        lane = lanes_of(rows)
        parts = []
        for i in range(4):
            pair[i, pl.ds(0, 2 * rows), :] = make(i)
            t = pair[i, pl.ds(0, rows, stride=2), :] + pair[i, pl.ds(1, rows, stride=2), :]
            parts.append(t + roll(t, 64))
        index = 2 * (lane & 31) + ((lane & 32) * 2)
        halves = []
        for i in (0, 2):
            t = jnp.where(lane < 64, parts[i], parts[i + 1])
            halves.append(pick(t, index) + pick(t, index + 1))
        return 0.125 * jnp.where(lane < 64, halves[0], halves[1])

    def restrict_2(make):
        def one(i):
            pair[i, pl.ds(0, 24), :] = make(i)
            t = pair[i, pl.ds(0, 12, stride=2), :] + pair[i, pl.ds(1, 12, stride=2), :]
            t = t + roll(t, -32)
            t = t + roll(t, -1)
            return 0.125 * pick(t, lanes_of(12) & ~33)

        return one

    def restrict_3(make):
        k = lanes_of(1) & 15
        row = None
        for i in range(8):
            pair[i, pl.ds(0, 4), :] = make(i)
            t = pair[i, pl.ds(0, 2, stride=2), :] + pair[i, pl.ds(1, 2, stride=2), :]
            t = t + roll(t, 64)
            t = 0.125 * pick(t + roll(t, -2), (lanes_of(2) >> 4) * 4)
            for j in range(2):
                row = t[j : j + 1] if row is None else jnp.where(k == 2 * i + j, t[j : j + 1], row)
        return row

    load_b.wait()


    pl.semaphore_wait(barrier, len(greeted))

    def pass_on(n, targets):
        for target in targets:
            pl.semaphore_signal(ready.at[n], inc=1, device_id=target, device_id_type=MESH)


    def cut(d, first, size, width):
        if d == 0:
            return first, first, size
        if d > 0:
            return first + size - width, first - width, width
        return first, first + size, width

    def send_near(slot, ref, blocks, rows, block_width, row_width):
        for dg, dq in near:
            bs, bt, bn = cut(dg, blocks[0], blocks[1], block_width)
            rs, rt, rn = cut(dq, rows[0], rows[1], row_width)
            copy = pltpu.make_async_remote_copy(
                src_ref=ref.at[pl.ds(bs, bn), pl.ds(rs, rn)],
                dst_ref=ref.at[pl.ds(bt, bn), pl.ds(rt, rn)],
                send_sem=send_sem.at[slot],
                recv_sem=recv_sem.at[slot],
                device_id=device(dg, dq),
                device_id_type=MESH,
            )
            copy.start()

    def all_of(sem, shape):
        some = l0.w.at[(0,) + tuple(pl.ds(0, n) for n in shape)]
        return pltpu.make_async_copy(some, some, sem)

    def arrive(group):
        all_of(recv_sem.at[group], GROUP_ROWS[group]).wait()

    send_near(0, l0.b, (3, 16), (O0, 32), 3, 3)
    load_f.wait()
    send_near(1, l0.f, (3, 16), (O0, 32), 2, 2)
    pass_on(
        0,
        [device(dg, dq) for dg in (-2, 2) for dq in (-1, 0, 1)]
        + [device_xz(0, dz) for dz in (3, -3)],
    )

    def clear(ref, blocks, rows, total_blocks, block_width, row_width):
        first, count = blocks
        start, height = rows

        @pl.when(g == 0)
        def _():
            for i in range(first - block_width, first):
                ref[i] = jnp.zeros(ref.shape[1:], F32)

        @pl.when(g == NG - 1)
        def _():
            for i in range(first + count, first + count + block_width):
                ref[i] = jnp.zeros(ref.shape[1:], F32)

        @pl.when(q == 0)
        def _():
            for i in range(first - block_width, first + count + block_width):
                ref[i, pl.ds(start - row_width, row_width), :] = jnp.zeros((row_width, 128), F32)

        @pl.when(q == NQ - 1)
        def _():
            for i in range(first - block_width, first + count + block_width):
                ref[i, pl.ds(start + height, row_width), :] = jnp.zeros((row_width, 128), F32)

    def store_b1(i, v):
        l1.b[3 + i, pl.ds(O1, 16), :] = v

    each(0, 4, restrict_0(lambda p: l0.b[3 + p, pl.ds(O0, 32), :], store_b1), 2)
    send_near(2, l1.b, (3, 4), (O1, 16), 2, 4)

    core = l0.window(14, 28)
    each(4, 18, core.weigh, 7)
    each(4, 18, core.first, 7)
    core = l0.window(16, 24)
    each(5, 17, lambda i: core.store(l0.u, i, core.smooth(l0.v, i)), 6)
    rims = (l0.window(8, 8), l0.window(40, 8))

    def outside(lo, width, hi, work):
        def rim(i):
            for one in rims:
                work(one, i)

        each(lo + width, hi - width, rim, (hi - lo - 2 * width) // 2)
        for i in list(range(lo, lo + width)) + list(range(hi - width, hi)):
            work(l0, i)

    arrive(0)
    clear(l0.b, (3, 16), (O0, 32), 22, 3, 3)
    outside(1, 3, 21, lambda one, i: one.weigh(i))
    arrive(1)
    outside(1, 3, 21, lambda one, i: one.first(i))
    outside(2, 3, 20, lambda one, i: one.store(l0.u, i, one.smooth(l0.v, i)))

    def store_f1(i, v):
        l1.f[3 + i, pl.ds(O1, 16), :] = v

    each(0, 4, restrict_0(lambda p: l0.residual(3 + p)[O0 - 8 : O0 - 8 + 32], store_f1), 2)
    send_near(3, l1.f, (3, 4), (O1, 16), 2, 4)

    arrive(2)
    clear(l1.b, (3, 4), (O1, 16), 10, 2, 4)
    b2_own[pl.ds(7, 10), :] = restrict_1(lambda i: l1.b[3 + i, pl.ds(O1 - 2, 20), :], 10)

    def send_wide(slot, parts):
        for dg, dq in wide:
            src, dst = parts(dq)
            copy = pltpu.make_async_remote_copy(
                src_ref=src,
                dst_ref=dst,
                send_sem=send_sem.at[slot],
                recv_sem=recv_sem.at[slot],
                device_id=device(dg, dq),
                device_id_type=MESH,
            )
            copy.start()

    pl.semaphore_wait(ready.at[0], 8)

    def b2_parts(dq):
        src, dst, n = {0: (8, O2, 8), 1: (7, O2 - 9, 9), -1: (8, O2 + 8, 9)}[dq]
        return b2_own.at[pl.ds(src, n)], l2.b.at[1 + g, pl.ds(dst, n)]

    send_wide(4, b2_parts)
    pass_on(1, [device_xz(dx, dz) for dx in range(4) for dz in (3, -3)])
    l2.b[1 + g, pl.ds(O2, 8), :] = b2_own[pl.ds(8, 8), :]
    each(1, 9, l1.weigh)
    arrive(3)
    each(1, 9, l1.first)
    each(2, 8, lambda i: l1.store(l1.u, i, l1.smooth(l1.v, i)))
    f2_own[...] = restrict_1(lambda i: l1.residual(3 + i)[O1 - 8 : O1 - 8 + 16], 8)

    def f2_parts(dq):
        return f2_own, l2.f.at[1 + g, pl.ds(O2 - 8 * dq, 8)]

    send_wide(5, f2_parts)
    l2.f[1 + g, pl.ds(O2, 8), :] = f2_own[...]

    arrive(4)

    @pl.when(q == 0)
    def _():
        for i in range(1, 9):
            l2.b[i, pl.ds(O2 - 9, 9), :] = jnp.zeros((9, 128), F32)

    @pl.when(q == NQ - 1)
    def _():
        for i in range(1, 9):
            l2.b[i, pl.ds(O2 + 8, 9), :] = jnp.zeros((9, 128), F32)

    each(1, 9, l2.weigh)
    b3_of = restrict_2(lambda i: l2.load(l2.b, i))

    def store_b3(i):
        l3.b[i, pl.ds(O3 - 4, 12), :] = b3_of(i)

    each(1, 9, store_b3)
    each(1, 9, l3.weigh)

    def send_rows(slot, ref, start, count, targets):
        here = ref.at[pl.ds(start, count)]
        for target in targets:
            copy = pltpu.make_async_remote_copy(
                src_ref=here,
                dst_ref=here,
                send_sem=send_sem.at[slot],
                recv_sem=recv_sem.at[slot],
                device_id=target,
                device_id_type=MESH,
            )
            copy.start()

    b4 = restrict_3(lambda i: l3.b[1 + i, pl.ds(O3, 4), :])
    pl.semaphore_wait(ready.at[1], 8)
    all_b4[pl.ds(q, 1), :] = b4
    send_rows(6, all_b4, q, 1, [device_xz(0, dz) for dz in (8, 7, 9, 6, 10, 5, 11, 4, 12, 3, 13, 2, 14, 1, 15)])

    arrive(5)
    each(1, 9, l2.first)
    each(1, 9, lambda i: l2.store(l2.u, i, l2.smooth(l2.v, i)))
    f3_of = restrict_2(l2.residual)

    def store_f3(i):
        l3.f[i, pl.ds(O3 - 4, 12), :] = f3_of(i)

    each(1, 9, store_f3)
    each(1, 9, l3.first)
    each(1, 9, lambda i: l3.store(l3.u, i, l3.smooth(l3.v, i)))
    f4 = restrict_3(lambda i: l3.residual(1 + i)[O3 - 8 : O3 - 8 + 4])

    all_f4[pl.ds(q, 1), :] = f4
    send_rows(7, all_f4, q, 1, [device(0, d) for d in far])
    arrive(6)
    send_rows(8, all_b4, pl.multiple_of((q >> 4) * 16, 16), 16, [device_xz(dx, 0) for dx in (2, 1, 3)])
    arrive(8)
    weight = all_b4[...]
    lane = lanes_of(NQ)
    row = lax.broadcasted_iota(jnp.int32, (NQ, 128), 0)
    odd = (lane & 1) == 1
    edges = (
        (lane & 14) == 14,
        (lane & 14) == 0,
        (row == NQ - 1) & odd,
        (row == 0) & jnp.logical_not(odd),
        lane >= 112,
        lane < 16,
    )

    def bottom_shifts(v):
        up, down = roll(v, -1), roll(v, 1)
        yp = jnp.where(odd, pltpu.roll(down, NQ - 1, 0), up)
        ym = jnp.where(odd, down, pltpu.roll(up, 1, 0))
        return roll(v, -2), roll(v, 2), yp, ym, roll(v, -16), roll(v, 16)

    half = 0.5 * 0.25**4
    bottom_w = []
    bottom_d = None
    for edge, other in zip(edges, bottom_shifts(weight)):
        w = half * (weight + jnp.where(edge, 0.0, other))
        bottom_d = w if bottom_d is None else bottom_d + w
        bottom_w.append(jnp.where(edge, 0.0, w))

    arrive(7)
    source = all_f4[...]

    def apply_op(v):
        result = bottom_d * v
        for w, other in zip(bottom_w, bottom_shifts(v)):
            result = result - w * other
        return result

    def total(v):
        return jnp.sum(v, keepdims=True)

    answer = None
    residual = source
    direction = source
    applied = None
    rho = total(source * source)
    alpha = omega = shadow_bent = None
    for turn in range(BITERS):
        if turn > 0:
            beta = -(alpha * shadow_bent) / rho
            rho = -(omega * shadow_bent)
            direction = residual + beta * (direction - omega * applied)
        applied = apply_op(direction)
        alpha = rho / total(source * applied)
        middle = residual - alpha * applied
        bent = apply_op(middle)
        omega = total(bent * middle) / total(bent * bent)
        shadow_bent = total(source * bent)
        step = alpha * direction + omega * middle
        answer = step if answer is None else answer + step
        residual = middle - omega * bent

    e_pad[pl.ds(8, NQ), :] = answer
    fine = lax.broadcasted_iota(jnp.int32, (16, 128), 0) - 8
    near_rows = jnp.where(
        fine < 0,
        e_pad[pl.ds(7 + q, 1), :],
        jnp.where(fine < 4, e_pad[pl.ds(8 + q, 1), :], e_pad[pl.ds(9 + q, 1), :]),
    )
    parity = jnp.where((fine < 0) | ((fine >= 2) & (fine < 4)), 1, 0)
    group = ((lanes_of(16) >> 2) & 7) * 16

    def up_3(i):
        wide_e = pick(near_rows, group + parity + 2 * (i - 1))
        l3.store(l3.v, i, l3.load(l3.u, i) + wide_e)

    each(1, 9, up_3)

    def up_3s(i):
        v = l3.smooth(l3.v, i)
        v = v[6:14]
        for k in range(2):
            pair[i, pl.ds(k, 8, stride=2), :] = v
        mid = l2.u[i, pl.ds(O2 - 4, 16), :] + pair[i, pl.ds(0, 16), :]
        l2.v[i, pl.ds(O2 - 4, 16), :] = mid

    each(1, 9, up_3s)
    each(1, 9, lambda i: l2.store(l2.u, i, l2.smooth(l2.v, i)))

    spread = (lanes_of(12) & 63) >> 1
    for i in range(-1, 5):
        from_block = 1 + g + (i // 4)
        v = pick(l2.u[from_block, pl.ds(O2 - 2, 12), :], spread + 32 * (i % 4))
        for k in range(2):
            pair[i + 1, pl.ds(k, 12, stride=2), :] = v
        l1.v[3 + i, pl.ds(O1 - 4, 24), :] = l1.u[3 + i, pl.ds(O1 - 4, 24), :] + pair[i + 1, pl.ds(0, 24), :]
    for i in range(-1, 5):
        l1.store(l1.u, 3 + i, l1.smooth(l1.v, 3 + i))

    spread = lanes_of(20) >> 1
    for i in range(-1, 9):
        v = l1.u[3 + (i // 2), pl.ds(O1 - 2, 20), :]
        v = pick(v, spread + 64 * (i % 2))
        for k in range(2):
            pair[i + 1, pl.ds(k, 20, stride=2), :] = v
        wide_v = pair[i + 1, pl.ds(0, 40), :]
        for p in (2 * i, 2 * i + 1):
            if -1 <= p <= 16:
                l0.store(l0.v, 3 + p, l0.load(l0.u, 3 + p) + wide_v)

    def finish(p):
        out[p] = l0.smooth(l0.v, 3 + p)[O0 - 8 : O0 - 8 + 32]

    each(0, 16, finish, 8)

    for group, shape in enumerate(GROUP_ROWS):
        all_of(send_sem.at[group], shape).wait()


def per_device(right_side, coefficient):
    scratch = []
    for blocks, rows in LEVEL_SHAPES:
        scratch += [pltpu.VMEM((blocks, rows, 128), F32)] * 6
        scratch.append(pltpu.VMEM((6, blocks, rows, 128), F32))
    scratch += [
        pltpu.VMEM((16, 48, 128), F32),
        pltpu.VMEM((24, 128), F32),
        pltpu.VMEM((8, 128), F32),
        pltpu.VMEM((NQ, 128), F32),
        pltpu.VMEM((NQ, 128), F32),
        pltpu.VMEM((80, 128), F32),
        pltpu.SemaphoreType.DMA((2,)),
        pltpu.SemaphoreType.DMA((9,)),
        pltpu.SemaphoreType.DMA((9,)),
        pltpu.SemaphoreType.REGULAR((2,)),
    ]
    return pl.pallas_call(
        kernel,
        out_shape=jax.ShapeDtypeStruct((16, 32, 128), F32),
        in_specs=[pl.BlockSpec(memory_space=pltpu.HBM)] * 2,
        out_specs=pl.BlockSpec(memory_space=pltpu.VMEM),
        scratch_shapes=scratch,
        compiler_params=pltpu.CompilerParams(
            collective_id=0, has_side_effects=True, vmem_limit_bytes=24 * 2**20
        ),
        cost_estimate=pl.CostEstimate(flops=10_000_000, bytes_accessed=3 * 262144, transcendentals=0),
    )(pltpu.with_memory_space_constraint(right_side, pltpu.HBM), pltpu.with_memory_space_constraint(coefficient, pltpu.HBM))


def solution(mesh):
    return jax.shard_map(
        per_device,
        mesh=mesh,
        in_specs=(P("gx", "yz", None), P("gx", "yz", None)),
        out_specs=P("gx", "yz", None),
        check_vma=False,
    )
```
